256 devices in a mesh: seq: 32 (over z, x_lo, core), fsdp: 8 (over y, x_hi).
Axes of the slice: x: 4 (x_hi: 2, x_lo: 2; x = x_hi * 2 + x_lo), y: 4, z: 8, core: 2. Of those that a mesh axis runs over, the one named last changes fastest.
Arguments:
- query_rows: bfloat16 [4096, 3072], P('seq', 'fsdp'), may hold values from -7 to 7
- key_rows: bfloat16 [4096, 3072], P('seq', 'fsdp'), may hold values from -7 to 7
- value_rows: bfloat16 [4096, 3072], P('seq', 'fsdp'), may hold values from -6 to 6
- tile_mask: int32 [32, 32], replicated, may hold values from 0 to 1, as said below
- up_weight: bfloat16 [3072, 10240], P('seq', 'fsdp'), may hold values from -0.109375 to 0.109375
- cotangent: bfloat16 [4096, 10240], P('seq', 'fsdp'), may hold values from -48 to 48
Outputs:
- scaled_act: bfloat16 [4096, 10240], P('seq', 'fsdp')
- grad_query: float32 [4096, 3072], P('seq', 'fsdp')
- grad_key: float32 [4096, 3072], P('seq', 'fsdp')
- grad_value: float32 [4096, 3072], P('seq', 'fsdp')
The draws below stay inside these ranges and needn't reach their ends.
Inputs may be any that keep to these rules, and one draw needn't show every extreme that they name: Tiles are numbered slab by slab and within a slab row by row over 2 x 2 tiles. tile_mask[i, j] is 1 exactly where tile j's slab is at most one away from tile i's, its row at most a distance of 0 or 1 (drawn for each tile i) from tile i's row, and its column at most a distance of 0 or 1 (drawn for each tile i) from tile i's column; 0 elsewhere.
All inputs are finite; a program needn't handle non-finite values.
Results may differ from the reference program's by a relative error of at most 0.022.
Values may be sent and summed in bfloat16 or wider, within the bound.
No kernel may reach another device: no remote copies, remote signals or barrier semaphores. Data moves between devices by JAX's collectives and lax.ppermute only.
A program may use at most 64 MiB of HBM per device.

```python
import jax
import jax.numpy as jnp
from jax import lax

HD = 128
HEADS = 24
D = 3072
FF = 10240
TILE = 128
GH = 2
GW = 2
TILES_DEV = 1
NTILES = 32
TOKENS = 4096
N_SEQ = 32
N_FSDP = 8


def rising_scale(low_end):
    position = jnp.arange(TOKENS, dtype=jnp.float32) / (TOKENS - 1)
    return (low_end + position)[:, None]


def draw_query_rows(key, part):
    key = jax.random.fold_in(key, 1)
    drawn = jnp.clip(jax.random.normal(key, (TOKENS, HEADS * HD), jnp.float32), -4.0, 4.0)
    return drawn.astype(jnp.bfloat16)


def draw_key_rows(key, part):
    key = jax.random.fold_in(key, 2)
    drawn = jnp.clip(jax.random.normal(key, (TOKENS, HEADS * HD), jnp.float32), -4.0, 4.0)
    return drawn.astype(jnp.bfloat16)


def draw_value_rows(key, part):
    key = jax.random.fold_in(key, 3)
    drawn = jnp.clip(jax.random.normal(key, (TOKENS, HEADS * HD), jnp.float32), -4.0, 4.0) * rising_scale(0.5)
    return drawn.astype(jnp.bfloat16)


def draw_cotangent(key, part):
    key = jax.random.fold_in(key, 4)
    drawn = jnp.clip(jax.random.normal(key, (TOKENS, FF), jnp.float32), -4.0, 4.0) * 8.0 * rising_scale(0.5)
    return drawn.astype(jnp.bfloat16)


def draw_tile_mask(key, part):
    key = jax.random.fold_in(key, 5)
    tile_ids = jnp.arange(NTILES, dtype=jnp.int32)
    slab_pos = tile_ids // (GH * GW)
    row_pos = tile_ids // GW % GH
    col_pos = tile_ids % GW
    row_reach = jax.random.randint(jax.random.fold_in(key, 1), (NTILES,), 0, 2)
    col_reach = jax.random.randint(jax.random.fold_in(key, 2), (NTILES,), 0, 2)
    near_slab = jnp.abs(slab_pos[:, None] - slab_pos[None, :]) <= 1
    near_rows = jnp.abs(row_pos[:, None] - row_pos[None, :]) <= row_reach[:, None]
    near_cols = jnp.abs(col_pos[:, None] - col_pos[None, :]) <= col_reach[:, None]
    return (near_slab & near_rows & near_cols).astype(jnp.int32)


def shard_levels(key, shape, cuts, smallest, top_value):
    def one(dim, blocks):
        heights = jax.random.uniform(jax.random.fold_in(jax.random.fold_in(key, 6), dim), (blocks,), jnp.float32, smallest / len(cuts), top_value / len(cuts))
        return jnp.repeat(jnp.exp(heights), shape[dim] // blocks).reshape((-1,) + (1,) * (len(shape) - dim - 1))

    factor_of = one(*cuts[0])
    for cut in cuts[1:]:
        factor_of = factor_of * one(*cut)
    return factor_of


def normal_values(own_key, shape, spread, limit, cuts=(), kind=jnp.bfloat16):
    loudness = shard_levels(own_key, shape, cuts, -0.22, 0.18) if cuts else 1.0
    result = jax.random.normal(own_key, shape, jnp.float32) * spread * loudness
    return jnp.minimum(jnp.maximum(result, -limit), limit).astype(kind)


def setup_inputs(seed: int = 0) -> dict:
    streams_of = jax.random.split(jax.random.key(seed), 7)
    return {
        "query_rows": draw_query_rows(jax.random.fold_in(streams_of[6], 71), 0),
        "key_rows": draw_key_rows(jax.random.fold_in(streams_of[6], 71), 0),
        "value_rows": draw_value_rows(jax.random.fold_in(streams_of[6], 71), 0),
        "tile_mask": draw_tile_mask(jax.random.fold_in(streams_of[6], 71), 0),
        "up_weight": normal_values(streams_of[4], (D, FF), D ** -0.5, 0.109375, ((0, 32), (1, 8))),
        "cotangent": draw_cotangent(jax.random.fold_in(streams_of[6], 71), 0),
    }


MASKED = -1e+30
EPSILON = 1e-05

def gelu_tanh(values):
    return jax.nn.gelu(values, approximate=True)

def widen_mask(mask_block):
    query_tiles, key_tiles = mask_block.shape
    grown_mask = jnp.broadcast_to((mask_block > 0)[:, None, :, None], (query_tiles, TILE, key_tiles, TILE))
    return grown_mask.reshape(query_tiles * TILE, key_tiles * TILE)

def round_trip(values):
    return lax.optimization_barrier(values.astype(jnp.bfloat16)).astype(jnp.float32)

def reference(query_rows, key_rows, value_rows, tile_mask, up_weight, cotangent):
    row_count = TILE * TILES_DEV
    score_scale = HD ** (-0.5)
    exact = lax.Precision.HIGHEST
    query_heads = query_rows.astype(jnp.float32).reshape(TOKENS, HEADS, HD)
    key_heads = key_rows.astype(jnp.float32).reshape(TOKENS, HEADS, HD)
    value_heads = value_rows.astype(jnp.float32).reshape(TOKENS, HEADS, HD)
    shards = jnp.arange(N_SEQ, dtype=jnp.int32)

    def shard_probs(shard_index):
        part_query = lax.dynamic_slice_in_dim(query_heads, shard_index * row_count, row_count, 0)
        mask_block = lax.dynamic_slice_in_dim(tile_mask, shard_index * TILES_DEV, TILES_DEV, 0)
        allowed = widen_mask(mask_block)[None]
        scores = jnp.einsum('qhd,khd->hqk', part_query, key_heads, precision=exact) * score_scale
        scores = jnp.where(allowed, scores, MASKED)
        top_score = lax.optimization_barrier(jnp.max(scores, axis=-1, keepdims=True))
        row_total = lax.optimization_barrier(jnp.sum(jnp.where(allowed, jnp.exp(scores - top_score), 0.0), axis=-1, keepdims=True))
        log_total = top_score + jnp.log(row_total)
        weights = jnp.where(allowed, jnp.exp(scores - log_total), 0.0)
        return (part_query, weights)

    def forward_shard(shard_index):
        _, weights = shard_probs(shard_index)
        mixed_rows = jnp.einsum('hqk,khd->qhd', round_trip(weights), value_heads, precision=exact)
        return mixed_rows.reshape(row_count, HEADS * HD).astype(jnp.bfloat16)
    attn_out = lax.map(forward_shard, shards).reshape(TOKENS, HEADS * HD)
    hidden = jnp.dot(attn_out, up_weight, preferred_element_type=jnp.float32)
    activated, gelu_pull = jax.vjp(gelu_tanh, hidden)
    mean_power = lax.optimization_barrier(jnp.mean(activated * activated, axis=0))
    inv_scale = lax.rsqrt(mean_power + EPSILON)
    scaled_act = (activated * inv_scale).astype(jnp.bfloat16)
    grad_scaled = cotangent.astype(jnp.float32)
    grad_inv = lax.optimization_barrier(jnp.sum(grad_scaled * activated, axis=0))
    grad_power = grad_inv * -0.5 * inv_scale * inv_scale * inv_scale
    grad_act = grad_scaled * inv_scale + grad_power * (2.0 / TOKENS) * activated
    grad_hidden = gelu_pull(grad_act)[0].astype(jnp.bfloat16)
    group_size = FF // N_FSDP
    attn_sum = jnp.zeros((TOKENS, HEADS * HD), jnp.float32)
    for group_index in range(N_FSDP):
        low_col = group_index * group_size
        group_part = jnp.dot(grad_hidden[:, low_col:low_col + group_size], up_weight[:, low_col:low_col + group_size].T, preferred_element_type=jnp.float32)
        attn_sum = attn_sum + round_trip(group_part)
    attn_grad = attn_sum.astype(jnp.bfloat16)
    grad_heads = attn_grad.astype(jnp.float32).reshape(TOKENS, HEADS, HD)
    out_heads = attn_out.astype(jnp.float32).reshape(TOKENS, HEADS, HD)

    def backward_shard(loop_carry, shard_index):
        key_sum, value_sum = loop_carry
        part_query, weights = shard_probs(shard_index)
        part_grad = lax.dynamic_slice_in_dim(grad_heads, shard_index * row_count, row_count, 0)
        part_out = lax.dynamic_slice_in_dim(out_heads, shard_index * row_count, row_count, 0)
        row_delta = jnp.einsum('qhd,qhd->hq', part_grad, part_out, precision=exact)
        grad_prob = jnp.einsum('qhd,khd->hqk', part_grad, value_heads, precision=exact)
        dscores = round_trip(weights * (grad_prob - row_delta[:, :, None]))
        query_grads = jnp.einsum('hqk,khd->qhd', dscores, key_heads, precision=exact) * score_scale
        key_part = jnp.einsum('hqk,qhd->khd', dscores, part_query, precision=exact) * score_scale
        value_part = jnp.einsum('hqk,qhd->khd', round_trip(weights), part_grad, precision=exact)
        new_carry = (key_sum + round_trip(key_part), value_sum + round_trip(value_part))
        return (new_carry, query_grads.reshape(row_count, HEADS * HD))
    zero_rows = jnp.zeros((TOKENS, HEADS, HD), jnp.float32)
    (key_sum, value_sum), grad_rows = lax.scan(backward_shard, (zero_rows, zero_rows), shards)
    grad_query = grad_rows.reshape(TOKENS, HEADS * HD)
    grad_key = key_sum.reshape(TOKENS, HEADS * HD)
    grad_value = value_sum.reshape(TOKENS, HEADS * HD)
    return (scaled_act, grad_query, grad_key, grad_value)
```

```python
import functools

import jax
import jax.numpy as jnp
from jax import lax
from jax.experimental import pallas as pl
from jax.experimental.pallas import tpu as pltpu
from jax.sharding import Mesh, PartitionSpec as P

HD = 128
TILE = 128
TOKENS = 4096
EPSILON = 1e-05
MASKED = -1e30
ROOT = 0.7978845608028654
CUBIC = 0.044715
PLANES = 8
NEAR = ((0, 0), (0, -1), (0, 1), (1, 0), (1, -1), (1, 1))
SEQ = ("z", "xl", "core")
FSDP = ("y", "xh")
NT = (((1,), (1,)), ((), ()))
TN = (((0,), (0,)), ((), ()))
VMEM = pltpu.VMEM
SMEM = pltpu.SMEM


def dot(a, b, dims=(((1,), (0,)), ((), ()))):
    return lax.dot_general(a, b, dims, preferred_element_type=jnp.float32)


def attend_kernel(place, mask, query, near_a, near_b, out, probs):
    z, xl, core = place[0], place[1], place[2]
    me = 4 * z + 2 * xl + core

    def bias_row(other_core):
        parts = []
        for dx, dz in NEAR:
            plane = z + dz
            inside = (plane >= 0) & (plane < PLANES)
            tile = 4 * jnp.clip(plane, 0, PLANES - 1) + 2 * (xl if dx == 0 else 1 - xl) + (1 - core if other_core else core)
            value = jnp.where(inside & (mask[me, tile] > 0), 0.0, MASKED).astype(jnp.float32)
            parts.append(jnp.full((1, TILE), value, jnp.float32))
        return jnp.concatenate(parts, axis=1)

    bias_a, bias_b = bias_row(False), bias_row(True)
    width = near_a.shape[1] // 2
    half = near_a.shape[0]
    scale = HD ** (-0.5)
    for head in range(width // HD):
        cols = slice(head * HD, (head + 1) * HD)
        vcols = slice(width + head * HD, width + (head + 1) * HD)
        q = query[:, cols]
        s_a = dot(q, near_a[:, cols], NT) * scale + bias_a
        s_b = dot(q, near_b[:, cols], NT) * scale + bias_b
        top = jnp.maximum(jnp.max(s_a, axis=1, keepdims=True), jnp.max(s_b, axis=1, keepdims=True))
        e_a = jnp.exp(s_a - top)
        e_b = jnp.exp(s_b - top)
        inv = 1.0 / (jnp.sum(e_a, axis=1, keepdims=True) + jnp.sum(e_b, axis=1, keepdims=True))
        p_a = e_a * inv
        p_b = e_b * inv
        probs[head, :, :half] = p_a
        probs[head, :, half:] = p_b
        mixed = dot(p_a.astype(jnp.bfloat16), near_a[:, vcols]) + dot(p_b.astype(jnp.bfloat16), near_b[:, vcols])
        out[:, :, cols] = jnp.broadcast_to(mixed.astype(jnp.bfloat16)[None], (out.shape[0],) + mixed.shape)


def attend(place, mask, query, near_a, near_b, copies):
    rows, width = query.shape
    heads = width // HD
    keys = 2 * near_a.shape[0]
    return pl.pallas_call(
        attend_kernel,
        out_shape=(
            jax.ShapeDtypeStruct((copies, rows, width), jnp.bfloat16),
            jax.ShapeDtypeStruct((heads, rows, keys), jnp.float32),
        ),
        in_specs=[pl.BlockSpec(memory_space=SMEM)] * 2 + [pl.BlockSpec(memory_space=VMEM)] * 3,
        out_specs=(pl.BlockSpec(memory_space=VMEM),) * 2,
        compiler_params=pltpu.CompilerParams(vmem_limit_bytes=24 << 20),
        cost_estimate=pl.CostEstimate(flops=4 * rows * keys * width, bytes_accessed=8 << 20, transcendentals=heads * rows * keys),
    )(place, mask, query, near_a, near_b)


def up_kernel(rows_in, weight, cot, act_out, slope_out, sums, total):
    step = pl.program_id(0)
    part = dot(rows_in[0], weight[...])

    @pl.when(step == 0)
    def _():
        total[...] = part

    @pl.when(step > 0)
    def _():
        total[...] += part

    @pl.when(step == pl.num_programs(0) - 1)
    def _():
        width = total.shape[1]
        chunks = width // 128
        for r in range(chunks):
            cols = slice(r * 128, (r + 1) * 128)
            v = total[:, cols]
            t = jnp.tanh(ROOT * (v + CUBIC * (v * v * v)))
            act = 0.5 * v * (1.0 + t)
            act_out[:, cols] = act
            slope_out[:, cols] = 0.5 * (1.0 + t) + 0.5 * v * (1.0 - t * t) * (ROOT * (1.0 + 3.0 * CUBIC * (v * v)))
            power = jnp.sum(act * act, axis=0, keepdims=True)
            pull = jnp.sum(act * cot[:, cols].astype(jnp.float32), axis=0, keepdims=True)
            sums[:, r : r + 1, :] = jnp.broadcast_to(power[None], (sums.shape[0], 1, 128))
            sums[:, chunks + r : chunks + r + 1, :] = jnp.broadcast_to(pull[None], (sums.shape[0], 1, 128))
        rest = sums.shape[1] - 2 * chunks
        sums[:, 2 * chunks :, :] = jnp.zeros((sums.shape[0], rest, 128), jnp.float32)


def up(rows_in, weight, cot, copies):
    parts, rows, depth = rows_in.shape
    width = weight.shape[1]
    lines = -(-2 * (width // 128) // 8) * 8
    return pl.pallas_call(
        up_kernel,
        grid=(parts,),
        out_shape=(
            jax.ShapeDtypeStruct((rows, width), jnp.float32),
            jax.ShapeDtypeStruct((rows, width), jnp.float32),
            jax.ShapeDtypeStruct((copies, lines, 128), jnp.float32),
        ),
        in_specs=[
            pl.BlockSpec((1, rows, depth), lambda i: (i, 0, 0)),
            pl.BlockSpec((depth, width), lambda i: (i, 0)),
            pl.BlockSpec((rows, width), lambda i: (0, 0)),
        ],
        out_specs=(
            pl.BlockSpec((rows, width), lambda i: (0, 0)),
            pl.BlockSpec((rows, width), lambda i: (0, 0)),
            pl.BlockSpec((copies, lines, 128), lambda i: (0, 0, 0)),
        ),
        scratch_shapes=[pltpu.VMEM((rows, width), jnp.float32)],
        compiler_params=pltpu.CompilerParams(vmem_limit_bytes=24 << 20),
        cost_estimate=pl.CostEstimate(
            flops=2 * rows * width * parts * depth, bytes_accessed=weight.size * 2, transcendentals=rows * width
        ),
    )(rows_in, weight, cot)


def down_kernel(act, slope, cot, sums, weight, out, scaled, grad):
    @pl.when(pl.program_id(0) == 0)
    def _():
        chunks = act.shape[1] // 128
        total = jnp.sum(sums[...], axis=0)
        for r in range(chunks):
            cols = slice(r * 128, (r + 1) * 128)
            a = act[:, cols]
            c = cot[:, cols].astype(jnp.float32)
            inv = lax.rsqrt(total[r : r + 1, :] * (1.0 / TOKENS) + EPSILON)
            pull = total[chunks + r : chunks + r + 1, :]
            scaled[:, cols] = (a * inv).astype(jnp.bfloat16)
            back = pull * -0.5 * inv * inv * inv * (2.0 / TOKENS)
            grad[:, cols] = ((c * inv + back * a) * slope[:, cols]).astype(jnp.bfloat16)

    out[0] = dot(grad[...], weight[...], NT).astype(jnp.bfloat16)


def down(act, slope, cot, sums, weight, parts):
    rows, width = act.shape
    depth = weight.shape[0] // parts
    whole = lambda i: (0, 0)
    return pl.pallas_call(
        down_kernel,
        grid=(parts,),
        out_shape=(
            jax.ShapeDtypeStruct((parts, rows, depth), jnp.bfloat16),
            jax.ShapeDtypeStruct((rows, width), jnp.bfloat16),
        ),
        in_specs=[
            pl.BlockSpec((rows, width), whole),
            pl.BlockSpec((rows, width), whole),
            pl.BlockSpec((rows, width), whole),
            pl.BlockSpec(sums.shape, lambda i: (0, 0, 0)),
            pl.BlockSpec((depth, width), lambda i: (i, 0)),
        ],
        out_specs=(
            pl.BlockSpec((1, rows, depth), lambda i: (i, 0, 0)),
            pl.BlockSpec((rows, width), whole),
        ),
        scratch_shapes=[pltpu.VMEM((rows, width), jnp.bfloat16)],
        compiler_params=pltpu.CompilerParams(vmem_limit_bytes=24 << 20),
        cost_estimate=pl.CostEstimate(
            flops=2 * rows * width * parts * depth, bytes_accessed=weight.size * 2, transcendentals=0
        ),
    )(act, slope, cot, sums, weight)


def backward_kernel(query, near_a, near_b, attn, probs, partial, grad_query, grad_a, grad_b):
    width = query.shape[1]
    half = near_a.shape[0]
    scale = HD ** (-0.5)
    for head in range(width // HD):
        cols = slice(head * HD, (head + 1) * HD)
        vcols = slice(width + head * HD, width + (head + 1) * HD)
        grad = partial[0, :, cols].astype(jnp.float32)
        for i in range(1, partial.shape[0]):
            grad = grad + partial[i, :, cols].astype(jnp.float32)
        g = grad.astype(jnp.bfloat16)
        delta = jnp.sum(g.astype(jnp.float32) * attn[0, :, cols].astype(jnp.float32), axis=1, keepdims=True)
        q = query[:, cols]
        out = None
        for side, (near, result) in enumerate(((near_a, grad_a), (near_b, grad_b))):
            p = probs[head, :, side * half : (side + 1) * half]
            d = (p * (dot(g, near[:, vcols], NT) - delta)).astype(jnp.bfloat16)
            term = dot(d, near[:, cols])
            out = term if out is None else out + term
            result[:, cols] = (dot(d, q, TN) * scale).astype(jnp.bfloat16)
            result[:, vcols] = dot(p.astype(jnp.bfloat16), g, TN).astype(jnp.bfloat16)
        grad_query[:, cols] = out * scale


def backward(query, near_a, near_b, attn, probs, partial):
    rows, width = query.shape
    copies = attn.shape[0]
    return pl.pallas_call(
        backward_kernel,
        grid=(1,),
        out_shape=(
            jax.ShapeDtypeStruct((rows, width), jnp.float32),
            jax.ShapeDtypeStruct(near_a.shape, jnp.bfloat16),
            jax.ShapeDtypeStruct(near_b.shape, jnp.bfloat16),
        ),
        in_specs=[
            pl.BlockSpec(query.shape, lambda i: (0, 0)),
            pl.BlockSpec(near_a.shape, lambda i: (0, 0)),
            pl.BlockSpec(near_b.shape, lambda i: (0, 0)),
            pl.BlockSpec((1,) + attn.shape[1:], lambda i: (0, 0, 0)),
            pl.BlockSpec(probs.shape, lambda i: (0, 0, 0)),
            pl.BlockSpec(partial.shape, lambda i: (0, 0, 0)),
        ],
        out_specs=(
            pl.BlockSpec((rows, width), lambda i: (0, 0)),
            pl.BlockSpec(near_a.shape, lambda i: (0, 0)),
            pl.BlockSpec(near_b.shape, lambda i: (0, 0)),
        ),
        compiler_params=pltpu.CompilerParams(vmem_limit_bytes=32 << 20),
        cost_estimate=pl.CostEstimate(
            flops=8 * rows * 2 * near_a.shape[0] * width, bytes_accessed=8 << 20, transcendentals=0
        ),
    )(query, near_a, near_b, attn, probs, partial)


def swap(value, axis):
    return lax.ppermute(value, axis, [(0, 1), (1, 0)])


def up_plane(value):
    return lax.ppermute(value, "z", [(i, (i + 1) % PLANES) for i in range(PLANES)])


def down_plane(value):
    return lax.ppermute(value, "z", [(i, (i - 1) % PLANES) for i in range(PLANES)])


def body(query, key, value, tile_mask, weight, cot):
    rows, width = query.shape
    place = jnp.stack([lax.axis_index("z"), lax.axis_index("xl"), lax.axis_index("core")]).astype(jnp.int32)
    full_weight = lax.all_gather(weight, SEQ, axis=0, tiled=True)
    own = jnp.concatenate([key, value], axis=1)
    from_low = up_plane(own)
    from_high = down_plane(own)
    own_x = swap(own, "xl")
    far_x = swap(jnp.concatenate([from_low, from_high], axis=0), "xl")
    near_a = jnp.concatenate([own, from_low, from_high, own_x, far_x], axis=0)
    near_b = swap(near_a, "core")
    copies = lax.axis_size(FSDP)
    attn, probs = attend(place, tile_mask, query, near_a, near_b, copies)
    full_rows = lax.all_to_all(attn, FSDP, 0, 0)
    act, slope, sums = up(full_rows, full_weight, cot, lax.axis_size(SEQ))
    sums = lax.all_to_all(sums, SEQ, 0, 0)
    back, scaled = down(act, slope, cot, sums, full_weight, copies)
    partial = lax.all_to_all(back, FSDP, 0, 0)
    grad_query, grad_a, grad_b = backward(query, near_a, near_b, attn, probs, partial)
    f32 = jnp.float32
    grad_a = grad_a.astype(f32) + swap(grad_b, "core").astype(f32)
    side = grad_a[3 * rows :].astype(jnp.bfloat16)
    mine = grad_a[: 3 * rows] + swap(side, "xl").astype(f32)
    far = mine[rows:].astype(jnp.bfloat16)
    grad_own = mine[:rows] + down_plane(far[:rows]).astype(f32) + up_plane(far[rows:]).astype(f32)
    return scaled, grad_query, grad_own[:, :width], grad_own[:, width:]


def solution(mesh):
    fine = Mesh(mesh.devices.reshape(PLANES, 2, 2, 4, 2), SEQ + FSDP)
    both = P(SEQ, FSDP)
    return jax.shard_map(
        body,
        mesh=fine,
        in_specs=(both, both, both, P(), both, both),
        out_specs=(both,) * 4,
        check_vma=False,
    )
```

```python
import functools

import jax
import jax.numpy as jnp
from jax import lax
from jax.experimental import pallas as pl
from jax.experimental.pallas import tpu as pltpu
from jax.sharding import Mesh, PartitionSpec as P

HD = 128
TILE = 128
TOKENS = 4096
EPSILON = 1e-05
MASKED = -1e30
ROOT = 0.7978845608028654
CUBIC = 0.044715
PLANES = 8
NEAR = ((0, 0), (0, -1), (0, 1), (1, 0), (1, -1), (1, 1))
SEQ = ("z", "xl", "core")
FSDP = ("y", "xh")
NT = (((1,), (1,)), ((), ()))
TN = (((0,), (0,)), ((), ()))
VMEM = pltpu.VMEM
SMEM = pltpu.SMEM


def dot(a, b, dims=(((1,), (0,)), ((), ()))):
    return lax.dot_general(a, b, dims, preferred_element_type=jnp.float32)


def attend_kernel(place, mask, query, near_a, near_b, out, probs):
    z, xl, core = place[0], place[1], place[2]
    me = 4 * z + 2 * xl + core

    def bias_row(other_core):
        parts = []
        for dx, dz in NEAR:
            plane = z + dz
            inside = (plane >= 0) & (plane < PLANES)
            tile = 4 * jnp.clip(plane, 0, PLANES - 1) + 2 * (xl if dx == 0 else 1 - xl) + (1 - core if other_core else core)
            value = jnp.where(inside & (mask[me, tile] > 0), 0.0, MASKED).astype(jnp.float32)
            parts.append(jnp.full((1, TILE), value, jnp.float32))
        return jnp.concatenate(parts, axis=1)

    bias_a, bias_b = bias_row(False), bias_row(True)
    width = near_a.shape[1] // 2
    half = near_a.shape[0]
    scale = HD ** (-0.5)
    for head in range(width // HD):
        cols = slice(head * HD, (head + 1) * HD)
        vcols = slice(width + head * HD, width + (head + 1) * HD)
        q = query[:, cols]
        s_a = dot(q, near_a[:, cols], NT) * scale + bias_a
        s_b = dot(q, near_b[:, cols], NT) * scale + bias_b
        top = jnp.maximum(jnp.max(s_a, axis=1, keepdims=True), jnp.max(s_b, axis=1, keepdims=True))
        e_a = jnp.exp(s_a - top)
        e_b = jnp.exp(s_b - top)
        inv = 1.0 / (jnp.sum(e_a, axis=1, keepdims=True) + jnp.sum(e_b, axis=1, keepdims=True))
        p_a = e_a * inv
        p_b = e_b * inv
        probs[head, :, :half] = p_a
        probs[head, :, half:] = p_b
        mixed = dot(p_a.astype(jnp.bfloat16), near_a[:, vcols]) + dot(p_b.astype(jnp.bfloat16), near_b[:, vcols])
        out[:, :, cols] = jnp.broadcast_to(mixed.astype(jnp.bfloat16)[None], (out.shape[0],) + mixed.shape)


def attend(place, mask, query, near_a, near_b, copies):
    rows, width = query.shape
    heads = width // HD
    keys = 2 * near_a.shape[0]
    return pl.pallas_call(
        attend_kernel,
        out_shape=(
            jax.ShapeDtypeStruct((copies, rows, width), jnp.bfloat16),
            jax.ShapeDtypeStruct((heads, rows, keys), jnp.float32),
        ),
        in_specs=[pl.BlockSpec(memory_space=SMEM)] * 2 + [pl.BlockSpec(memory_space=VMEM)] * 3,
        out_specs=(pl.BlockSpec(memory_space=VMEM),) * 2,
        compiler_params=pltpu.CompilerParams(vmem_limit_bytes=24 << 20),
        cost_estimate=pl.CostEstimate(flops=4 * rows * keys * width, bytes_accessed=8 << 20, transcendentals=heads * rows * keys),
    )(place, mask, query, near_a, near_b)


def up_kernel(rows_in, weight, cot, act_out, slope_out, sums, held, total, arrived):
    parts, rows, depth = rows_in.shape
    width = held.shape[1]
    piece = weight.shape[3]
    copies = []
    for part in range(parts):
        for core in range(2):
            for xl in range(2):
                where = part * depth + (2 * xl + core) * piece
                copies.append(
                    pltpu.make_async_copy(
                        weight.at[part, core, xl], held.at[pl.ds(where, piece), :], arrived.at[part, 2 * core + xl]
                    )
                )
    for copy in copies:
        copy.start()
    for part in range(parts):
        for copy in copies[4 * part : 4 * part + 4]:
            copy.wait()
        term = dot(rows_in[part], held[part * depth : (part + 1) * depth, :])
        if part == 0:
            total[...] = term
        else:
            total[...] += term
    chunks = width // 128
    power, pull = [], []
    for r in range(chunks):
        cols = slice(r * 128, (r + 1) * 128)
        v = total[:, cols]
        t = jnp.tanh(ROOT * (v + CUBIC * (v * v * v)))
        act = 0.5 * v * (1.0 + t)
        act_out[:, cols] = act
        slope_out[:, cols] = 0.5 * (1.0 + t) + 0.5 * v * (1.0 - t * t) * (ROOT * (1.0 + 3.0 * CUBIC * (v * v)))
        power.append(jnp.sum(act * act, axis=0, keepdims=True))
        pull.append(jnp.sum(act * cot[:, cols].astype(jnp.float32), axis=0, keepdims=True))
    lines = power + pull + [jnp.zeros((sums.shape[1] - 2 * chunks, 128), jnp.float32)]
    sums[...] = jnp.broadcast_to(jnp.concatenate(lines, axis=0).astype(jnp.bfloat16)[None], sums.shape)


def up(rows_in, weight, cot, copies):
    parts, rows, depth = rows_in.shape
    width = weight.shape[1]
    lines = -(-2 * (width // 128) // 8) * 8
    in_vmem = pl.BlockSpec(memory_space=VMEM)
    return pl.pallas_call(
        up_kernel,
        out_shape=(
            jax.ShapeDtypeStruct((rows, width), jnp.float32),
            jax.ShapeDtypeStruct((rows, width), jnp.float32),
            jax.ShapeDtypeStruct((copies, lines, 128), jnp.bfloat16),
            VMEM(weight.shape, jnp.bfloat16),
        ),
        in_specs=[in_vmem, pl.BlockSpec(memory_space=pltpu.HBM), in_vmem],
        out_specs=(in_vmem,) * 4,
        scratch_shapes=[pltpu.VMEM((rows, width), jnp.float32), pltpu.SemaphoreType.DMA((parts, 4))],
        compiler_params=pltpu.CompilerParams(vmem_limit_bytes=40 << 20),
        cost_estimate=pl.CostEstimate(
            flops=2 * rows * width * parts * depth, bytes_accessed=weight.size * 2, transcendentals=rows * width
        ),
    )(rows_in, weight.reshape(parts, 2, 2, depth // 4, width), cot)


def down_kernel(act, slope, cot, sums, weight, out, scaled, grad):
    chunks = act.shape[1] // 128
    total = jnp.sum(sums[...].astype(jnp.float32), axis=0)
    for r in range(chunks):
        cols = slice(r * 128, (r + 1) * 128)
        a = act[:, cols]
        c = cot[:, cols].astype(jnp.float32)
        inv = lax.rsqrt(total[r : r + 1, :] * (1.0 / TOKENS) + EPSILON)
        pull = total[chunks + r : chunks + r + 1, :]
        scaled[:, cols] = (a * inv).astype(jnp.bfloat16)
        back = pull * -0.5 * inv * inv * inv * (2.0 / TOKENS)
        grad[:, cols] = ((c * inv + back * a) * slope[:, cols]).astype(jnp.bfloat16)
    parts, _, depth = out.shape
    for part in range(parts):
        out[part] = dot(grad[...], weight[part * depth : (part + 1) * depth, :], NT).astype(jnp.bfloat16)


def down(act, slope, cot, sums, weight, parts):
    rows, width = act.shape
    depth = weight.shape[0] // parts
    in_vmem = pl.BlockSpec(memory_space=VMEM)
    return pl.pallas_call(
        down_kernel,
        out_shape=(
            jax.ShapeDtypeStruct((parts, rows, depth), jnp.bfloat16),
            jax.ShapeDtypeStruct((rows, width), jnp.bfloat16),
        ),
        in_specs=[in_vmem] * 5,
        out_specs=(in_vmem,) * 2,
        scratch_shapes=[pltpu.VMEM((rows, width), jnp.bfloat16)],
        compiler_params=pltpu.CompilerParams(vmem_limit_bytes=24 << 20),
        cost_estimate=pl.CostEstimate(
            flops=2 * rows * width * parts * depth, bytes_accessed=weight.size * 2, transcendentals=0
        ),
    )(act, slope, cot, sums, weight)


def backward_kernel(query, near_a, near_b, attn, probs, partial, grad_query, grad_a, grad_b):
    width = query.shape[1]
    half = near_a.shape[0]
    scale = HD ** (-0.5)
    for head in range(width // HD):
        cols = slice(head * HD, (head + 1) * HD)
        vcols = slice(width + head * HD, width + (head + 1) * HD)
        grad = partial[0, :, cols].astype(jnp.float32)
        for i in range(1, partial.shape[0]):
            grad = grad + partial[i, :, cols].astype(jnp.float32)
        g = grad.astype(jnp.bfloat16)
        delta = jnp.sum(g.astype(jnp.float32) * attn[0, :, cols].astype(jnp.float32), axis=1, keepdims=True)
        q = query[:, cols]
        out = None
        for side, (near, result) in enumerate(((near_a, grad_a), (near_b, grad_b))):
            p = probs[head, :, side * half : (side + 1) * half]
            d = (p * (dot(g, near[:, vcols], NT) - delta)).astype(jnp.bfloat16)
            term = dot(d, near[:, cols])
            out = term if out is None else out + term
            result[:, cols] = (dot(d, q, TN) * scale).astype(jnp.bfloat16)
            result[:, vcols] = dot(p.astype(jnp.bfloat16), g, TN).astype(jnp.bfloat16)
        grad_query[:, cols] = out * scale


def backward(query, near_a, near_b, attn, probs, partial):
    rows, width = query.shape
    copies = attn.shape[0]
    return pl.pallas_call(
        backward_kernel,
        grid=(1,),
        out_shape=(
            jax.ShapeDtypeStruct((rows, width), jnp.float32),
            jax.ShapeDtypeStruct(near_a.shape, jnp.bfloat16),
            jax.ShapeDtypeStruct(near_b.shape, jnp.bfloat16),
        ),
        in_specs=[
            pl.BlockSpec(query.shape, lambda i: (0, 0)),
            pl.BlockSpec(near_a.shape, lambda i: (0, 0)),
            pl.BlockSpec(near_b.shape, lambda i: (0, 0)),
            pl.BlockSpec((1,) + attn.shape[1:], lambda i: (0, 0, 0)),
            pl.BlockSpec(probs.shape, lambda i: (0, 0, 0)),
            pl.BlockSpec(partial.shape, lambda i: (0, 0, 0)),
        ],
        out_specs=(
            pl.BlockSpec((rows, width), lambda i: (0, 0)),
            pl.BlockSpec(near_a.shape, lambda i: (0, 0)),
            pl.BlockSpec(near_b.shape, lambda i: (0, 0)),
        ),
        compiler_params=pltpu.CompilerParams(vmem_limit_bytes=32 << 20),
        cost_estimate=pl.CostEstimate(
            flops=8 * rows * 2 * near_a.shape[0] * width, bytes_accessed=8 << 20, transcendentals=0
        ),
    )(query, near_a, near_b, attn, probs, partial)


def swap(value, axis):
    return lax.ppermute(value, axis, [(0, 1), (1, 0)])


def up_plane(value):
    return lax.ppermute(value, "z", [(i, (i + 1) % PLANES) for i in range(PLANES)])


def down_plane(value):
    return lax.ppermute(value, "z", [(i, (i - 1) % PLANES) for i in range(PLANES)])


def body(query, key, value, tile_mask, weight, cot):
    rows, width = query.shape
    f32, bf16 = jnp.float32, jnp.bfloat16
    xl = lax.axis_index("xl")
    place = jnp.stack([lax.axis_index("z"), xl, lax.axis_index("core")]).astype(jnp.int32)
    other = swap(weight, "xl")
    pair = jnp.concatenate([jnp.where(xl == 0, weight, other), jnp.where(xl == 0, other, weight)], axis=0)
    full_weight = lax.all_gather(pair, ("z", "core"), axis=0, tiled=True)
    own = jnp.concatenate([key, value], axis=1)
    from_low = up_plane(own)
    from_high = down_plane(own)
    own_x = swap(own, "xl")
    far_x = swap(jnp.concatenate([from_low, from_high], axis=0), "xl")
    near_a = jnp.concatenate([own, from_low, from_high, own_x, far_x], axis=0)
    near_b = swap(near_a, "core")
    copies = lax.axis_size(FSDP)
    attn, probs = attend(place, tile_mask, query, near_a, near_b, copies)
    full_rows = lax.all_to_all(attn, FSDP, 0, 0)
    act, slope, sums, held = up(full_rows, full_weight, cot, lax.axis_size(SEQ))
    sums = lax.all_to_all(sums, SEQ, 0, 0)
    back, scaled = down(act, slope, cot, sums, held, copies)
    partial = lax.all_to_all(back, FSDP, 0, 0)
    grad_query, grad_a, grad_b = backward(query, near_a, near_b, attn, probs, partial)
    both = (grad_a.astype(f32) + swap(grad_b, "core").astype(f32)).reshape(2, len(NEAR) // 2, rows, 2 * width)
    to_low, to_high = both[:, 1].astype(bf16), both[:, 2].astype(bf16)
    here = both[:, 0] + down_plane(to_low).astype(f32) + up_plane(to_high).astype(f32)
    grad_own = here[0] + swap(here[1].astype(bf16), "xl").astype(f32)
    return scaled, grad_query, grad_own[:, :width], grad_own[:, width:]


def solution(mesh):
    fine = Mesh(mesh.devices.reshape(PLANES, 2, 2, 4, 2), SEQ + FSDP)
    both = P(SEQ, FSDP)
    return jax.shard_map(
        body,
        mesh=fine,
        in_specs=(both, both, both, P(), both, both),
        out_specs=(both,) * 4,
        check_vma=False,
    )
```

```python
import functools

import jax
import jax.numpy as jnp
from jax import lax
from jax.experimental import pallas as pl
from jax.experimental.pallas import tpu as pltpu
from jax.sharding import Mesh, PartitionSpec as P

HD = 128
TILE = 128
TOKENS = 4096
EPSILON = 1e-05
MASKED = -1e30
ROOT = 0.7978845608028654
CUBIC = 0.044715
PLANES = 8
NEAR = ((0, 0), (1, 0), (0, -1), (1, -1), (0, 1), (1, 1))
SEQ = ("z", "xl", "core")
FSDP = ("y", "xh")
WIDE = ("xl", "y", "xh")
NT = (((1,), (1,)), ((), ()))
TN = (((0,), (0,)), ((), ()))
VMEM = pltpu.VMEM
SMEM = pltpu.SMEM


def dot(a, b, dims=(((1,), (0,)), ((), ()))):
    return lax.dot_general(a, b, dims, preferred_element_type=jnp.float32)


def attend_kernel(place, mask, query, near_a, near_b, out, plain, probs):
    z, xl, core = place[0], place[1], place[2]
    me = 4 * z + 2 * xl + core

    def bias_row(other_core):
        parts = []
        for dx, dz in NEAR:
            plane = z + dz
            inside = (plane >= 0) & (plane < PLANES)
            tile = 4 * jnp.clip(plane, 0, PLANES - 1) + 2 * (xl if dx == 0 else 1 - xl) + (1 - core if other_core else core)
            value = jnp.where(inside & (mask[me, tile] > 0), 0.0, MASKED).astype(jnp.float32)
            parts.append(jnp.full((1, TILE), value, jnp.float32))
        return jnp.concatenate(parts, axis=1)

    bias_a, bias_b = bias_row(False), bias_row(True)
    width = near_a.shape[1] // 2
    half = near_a.shape[0]
    scale = HD ** (-0.5)
    for head in range(width // HD):
        cols = slice(head * HD, (head + 1) * HD)
        vcols = slice(width + head * HD, width + (head + 1) * HD)
        q = query[:, cols]
        s_a = dot(q, near_a[:, cols], NT) * scale + bias_a
        s_b = dot(q, near_b[:, cols], NT) * scale + bias_b
        top = jnp.maximum(jnp.max(s_a, axis=1, keepdims=True), jnp.max(s_b, axis=1, keepdims=True))
        e_a = jnp.exp(s_a - top)
        e_b = jnp.exp(s_b - top)
        inv = 1.0 / (jnp.sum(e_a, axis=1, keepdims=True) + jnp.sum(e_b, axis=1, keepdims=True))
        p_a = e_a * inv
        p_b = e_b * inv
        probs[head, :, :half] = p_a
        probs[head, :, half:] = p_b
        mixed = dot(p_a.astype(jnp.bfloat16), near_a[:, vcols]) + dot(p_b.astype(jnp.bfloat16), near_b[:, vcols])
        mixed = mixed.astype(jnp.bfloat16)
        plain[:, cols] = mixed
        turned = mixed.astype(jnp.float32).T.astype(jnp.bfloat16)
        _, copies, lines, tokens = out.shape
        start = head * HD
        while start < (head + 1) * HD:
            side, low = divmod(start, lines)
            stop = min((head + 1) * HD, (side + 1) * lines)
            piece = turned[start - head * HD : stop - head * HD]
            out[side, :, low : low + stop - start, :] = jnp.broadcast_to(piece[None], (copies,) + piece.shape)
            start = stop


def attend(place, mask, query, near_a, near_b, copies):
    rows, width = query.shape
    heads = width // HD
    keys = 2 * near_a.shape[0]
    return pl.pallas_call(
        attend_kernel,
        out_shape=(
            jax.ShapeDtypeStruct((2, copies, width // 2, rows), jnp.bfloat16),
            jax.ShapeDtypeStruct((rows, width), jnp.bfloat16),
            jax.ShapeDtypeStruct((heads, rows, keys), jnp.float32),
        ),
        in_specs=[pl.BlockSpec(memory_space=SMEM)] * 2 + [pl.BlockSpec(memory_space=VMEM)] * 3,
        out_specs=(pl.BlockSpec(memory_space=VMEM),) * 3,
        compiler_params=pltpu.CompilerParams(vmem_limit_bytes=24 << 20),
        cost_estimate=pl.CostEstimate(flops=4 * rows * keys * width, bytes_accessed=8 << 20, transcendentals=heads * rows * keys),
    )(place, mask, query, near_a, near_b)


def up_kernel(place, rows_in, weight, cot, mine, theirs, held, cot_out, total, arrived):
    parts, depth, _ = weight.shape
    rows = rows_in.shape[2]
    own = place[1]
    copies = [pltpu.make_async_copy(weight.at[part], held.at[part], arrived.at[part]) for part in range(parts)]
    copies.append(pltpu.make_async_copy(cot, cot_out, arrived.at[parts]))
    for copy in copies:
        copy.start()
    group = 4
    for first in range(0, parts, group):
        for copy in copies[first : first + group]:
            copy.wait()
        near = rows_in[pl.ds(own * parts + first, group)].reshape(group * depth, rows)
        far = rows_in[pl.ds((1 - own) * parts + first, group)].reshape(group * depth, rows)
        held_rows = held[first : first + group].reshape(group * depth, held.shape[2])
        term = dot(jnp.concatenate([near, far], axis=1), held_rows, TN)
        if first == 0:
            total[...] = term
        elif first + group < parts:
            total[...] += term
        else:
            term = total[...] + term
            mine[...] = term[:rows]
            theirs[...] = term[rows:].astype(jnp.bfloat16)
    copies[parts].wait()


def up(place, rows_in, weight, cot):
    sides, depth, rows = rows_in.shape
    parts = sides // 2
    width = weight.shape[1]
    in_vmem = pl.BlockSpec(memory_space=VMEM)
    in_hbm = pl.BlockSpec(memory_space=pltpu.HBM)
    return pl.pallas_call(
        up_kernel,
        out_shape=(
            jax.ShapeDtypeStruct((rows, width), jnp.float32),
            jax.ShapeDtypeStruct((rows, width), jnp.bfloat16),
            VMEM((parts, depth, width), jnp.bfloat16),
            VMEM(cot.shape, jnp.bfloat16),
        ),
        in_specs=[pl.BlockSpec(memory_space=SMEM), in_vmem, in_hbm, in_hbm],
        out_specs=(in_vmem,) * 4,
        scratch_shapes=[pltpu.VMEM((2 * rows, width), jnp.float32), pltpu.SemaphoreType.DMA((parts + 1,))],
        compiler_params=pltpu.CompilerParams(vmem_limit_bytes=46 << 20),
        cost_estimate=pl.CostEstimate(
            flops=4 * rows * width * parts * depth, bytes_accessed=weight.size * 2, transcendentals=0
        ),
    )(place, rows_in, weight.reshape(parts, depth, width), cot)


def middle_kernel(mine, got, cot, act_out, pull_out, push_out, pair, sums):
    chunks = mine.shape[1] // 128
    power, pull = [], []
    for r in range(chunks):
        cols = slice(r * 128, (r + 1) * 128)
        v = mine[:, cols] + got[:, cols].astype(jnp.float32)
        t = jnp.tanh(ROOT * (v + CUBIC * (v * v * v)))
        act = 0.5 * v * (1.0 + t)
        slope = 0.5 * (1.0 + t) + 0.5 * v * (1.0 - t * t) * (ROOT * (1.0 + 3.0 * CUBIC * (v * v)))
        c = cot[:, cols].astype(jnp.float32)
        act_out[:, cols] = act
        pull_out[:, cols] = c * slope
        push_out[:, cols] = act * slope
        pair[0, :, cols] = (c * slope).astype(jnp.bfloat16)
        pair[1, :, cols] = (act * slope).astype(jnp.bfloat16)
        power.append(jnp.sum(act * act, axis=0, keepdims=True))
        pull.append(jnp.sum(act * c, axis=0, keepdims=True))
    lines = power + pull + [jnp.zeros((sums.shape[1] - 2 * chunks, 128), jnp.float32)]
    sums[...] = jnp.broadcast_to(jnp.concatenate(lines, axis=0).astype(jnp.bfloat16)[None], sums.shape)


def middle(mine, got, cot, copies):
    rows, width = mine.shape
    lines = -(-2 * (width // 128) // 8) * 8
    in_vmem = pl.BlockSpec(memory_space=VMEM)
    wide = jax.ShapeDtypeStruct((rows, width), jnp.float32)
    return pl.pallas_call(
        middle_kernel,
        out_shape=(
            wide,
            wide,
            wide,
            jax.ShapeDtypeStruct((2, rows, width), jnp.bfloat16),
            jax.ShapeDtypeStruct((copies, lines, 128), jnp.bfloat16),
        ),
        in_specs=[in_vmem] * 3,
        out_specs=(in_vmem,) * 5,
        compiler_params=pltpu.CompilerParams(vmem_limit_bytes=24 << 20),
        cost_estimate=pl.CostEstimate(flops=40 * rows * width, bytes_accessed=4 << 20, transcendentals=rows * width),
    )(mine, got, cot)


def down_kernel(place, act, pull, push, pair, sums, weight, out, scaled, grad):
    rows, width = act.shape
    chunks = width // 128
    own = place[1]
    total = jnp.sum(sums[...].astype(jnp.float32), axis=0)
    for r in range(chunks):
        cols = slice(r * 128, (r + 1) * 128)
        inv = lax.rsqrt(total[r : r + 1, :] * (1.0 / TOKENS) + EPSILON)
        back = total[chunks + r : chunks + r + 1, :] * -0.5 * inv * inv * inv * (2.0 / TOKENS)
        scaled[:, cols] = (act[:, cols] * inv).astype(jnp.bfloat16)
        grad[:rows, cols] = (pull[:, cols] * inv + back * push[:, cols]).astype(jnp.bfloat16)
        far = pair[0, :, cols].astype(jnp.float32) * inv + back * pair[1, :, cols].astype(jnp.float32)
        grad[rows:, cols] = far.astype(jnp.bfloat16)
    parts, depth, _ = weight.shape
    group = 4
    for first in range(0, parts, group):
        term = dot(weight[first : first + group].reshape(group * depth, width), grad[...], NT).astype(jnp.bfloat16)
        out[pl.ds(own * parts + first, group)] = term[:, :rows].reshape(group, depth, rows)
        out[pl.ds((1 - own) * parts + first, group)] = term[:, rows:].reshape(group, depth, rows)


def down(place, act, pull, push, pair, sums, weight):
    rows, width = act.shape
    parts, depth, _ = weight.shape
    in_vmem = pl.BlockSpec(memory_space=VMEM)
    return pl.pallas_call(
        down_kernel,
        out_shape=(
            jax.ShapeDtypeStruct((2 * parts, depth, rows), jnp.bfloat16),
            jax.ShapeDtypeStruct((rows, width), jnp.bfloat16),
        ),
        in_specs=[pl.BlockSpec(memory_space=SMEM)] + [in_vmem] * 6,
        out_specs=(in_vmem,) * 2,
        scratch_shapes=[pltpu.VMEM((2 * rows, width), jnp.bfloat16)],
        compiler_params=pltpu.CompilerParams(vmem_limit_bytes=24 << 20),
        cost_estimate=pl.CostEstimate(
            flops=4 * rows * width * parts * depth, bytes_accessed=weight.size * 2, transcendentals=0
        ),
    )(place, act, pull, push, pair, sums, weight)


def backward_kernel(query, near_a, near_b, attn, probs, partial, grad_query, grad_a, grad_b):
    width = query.shape[1]
    half = near_a.shape[0]
    scale = HD ** (-0.5)
    parts = partial.shape[0] // 2
    sides = []
    for side in range(2):
        total = partial[side * parts].astype(jnp.float32)
        for i in range(1, parts):
            total = total + partial[side * parts + i].astype(jnp.float32)
        sides.append(total)
    turned = jnp.concatenate(sides, axis=0)
    for head in range(width // HD):
        cols = slice(head * HD, (head + 1) * HD)
        vcols = slice(width + head * HD, width + (head + 1) * HD)
        g = turned[cols].T.astype(jnp.bfloat16)
        delta = jnp.sum(g.astype(jnp.float32) * attn[:, cols].astype(jnp.float32), axis=1, keepdims=True)
        q = query[:, cols]
        out = None
        for side, (near, result) in enumerate(((near_a, grad_a), (near_b, grad_b))):
            p = probs[head, :, side * half : (side + 1) * half]
            d = (p * (dot(g, near[:, vcols], NT) - delta)).astype(jnp.bfloat16)
            term = dot(d, near[:, cols])
            out = term if out is None else out + term
            result[:, cols] = (dot(d, q, TN) * scale).astype(jnp.bfloat16)
            result[:, vcols] = dot(p.astype(jnp.bfloat16), g, TN).astype(jnp.bfloat16)
        grad_query[:, cols] = out * scale


def backward(query, near_a, near_b, attn, probs, partial):
    rows, width = query.shape
    in_vmem = pl.BlockSpec(memory_space=VMEM)
    return pl.pallas_call(
        backward_kernel,
        out_shape=(
            jax.ShapeDtypeStruct((rows, width), jnp.float32),
            jax.ShapeDtypeStruct(near_a.shape, jnp.bfloat16),
            jax.ShapeDtypeStruct(near_b.shape, jnp.bfloat16),
        ),
        in_specs=[in_vmem] * 6,
        out_specs=(in_vmem,) * 3,
        compiler_params=pltpu.CompilerParams(vmem_limit_bytes=24 << 20),
        cost_estimate=pl.CostEstimate(
            flops=8 * rows * 2 * near_a.shape[0] * width, bytes_accessed=8 << 20, transcendentals=0
        ),
    )(query, near_a, near_b, attn, probs, partial)


def swap(value, axis):
    return lax.ppermute(value, axis, [(0, 1), (1, 0)])


def up_plane(value):
    return lax.ppermute(value, "z", [(i, (i + 1) % PLANES) for i in range(PLANES)])


def down_plane(value):
    return lax.ppermute(value, "z", [(i, (i - 1) % PLANES) for i in range(PLANES)])


def body(query, key, value, tile_mask, weight, cot):
    rows, width = query.shape
    f32, bf16 = jnp.float32, jnp.bfloat16
    place = jnp.stack([lax.axis_index("z"), lax.axis_index("xl"), lax.axis_index("core")]).astype(jnp.int32)
    half_weight = lax.all_gather(weight, ("z", "core"), axis=0, tiled=True)
    own = jnp.concatenate([key, value], axis=1)
    own = jnp.concatenate([own, swap(own, "xl")], axis=0)
    near_a = jnp.concatenate([own, up_plane(own), down_plane(own)], axis=0)
    near_b = swap(near_a, "core")
    attn_out, attn, probs = attend(place, tile_mask, query, near_a, near_b, lax.axis_size(FSDP))
    sides, copies, depth, _ = attn_out.shape
    rows_in = lax.all_to_all(attn_out.reshape(sides * copies, depth, rows), WIDE, 0, 0)
    mine, theirs, held, cot = up(place, rows_in, half_weight, cot)
    act, pull, push, pair, sums = middle(mine, swap(theirs, "xl"), cot, lax.axis_size(SEQ))
    pair = swap(pair, "xl")
    sums = lax.all_to_all(sums, SEQ, 0, 0)
    back, scaled = down(place, act, pull, push, pair, sums, held)
    partial = lax.all_to_all(back, WIDE, 0, 0)
    grad_query, grad_a, grad_b = backward(query, near_a, near_b, attn, probs, partial)
    both = (grad_a.astype(f32) + swap(grad_b, "core").astype(f32)).reshape(3, 2, rows, 2 * width)
    to_low, to_high = both[1].astype(bf16), both[2].astype(bf16)
    here = both[0] + down_plane(to_low).astype(f32) + up_plane(to_high).astype(f32)
    grad_own = here[0] + swap(here[1].astype(bf16), "xl").astype(f32)
    return scaled, grad_query, grad_own[:, :width], grad_own[:, width:]


def solution(mesh):
    fine = Mesh(mesh.devices.reshape(PLANES, 2, 2, 4, 2), SEQ + FSDP)
    both = P(SEQ, FSDP)
    return jax.shard_map(
        body,
        mesh=fine,
        in_specs=(both, both, both, P(), both, both),
        out_specs=(both,) * 4,
        check_vma=False,
    )
```

```python
import functools

import jax
import jax.numpy as jnp
from jax import lax
from jax.experimental import pallas as pl
from jax.experimental.pallas import tpu as pltpu
from jax.sharding import Mesh, PartitionSpec as P

HD = 128
TILE = 128
TOKENS = 4096
EPSILON = 1e-05
MASKED = -1e30
ROOT = 0.7978845608028654
CUBIC = 0.044715
PLANES = 8
GROUP = 4
NEAR = ((0, 0), (1, 0), (0, -1), (1, -1), (0, 1), (1, 1))
SEQ = ("z", "xl", "core")
FSDP = ("y", "xh")
WIDE = ("xl", "y", "xh")
NT = (((1,), (1,)), ((), ()))
TN = (((0,), (0,)), ((), ()))
VMEM = pltpu.VMEM
SMEM = pltpu.SMEM


def dot(a, b, dims=(((1,), (0,)), ((), ()))):
    return lax.dot_general(a, b, dims, preferred_element_type=jnp.float32)


def attend_kernel(place, mask, query, near_a, near_b, cot, out, plain, probs, cot_out, kept, sent):
    z, xl, core = place[0], place[1], place[2]
    me = 4 * z + 2 * xl + core

    def bias_row(other_core):
        parts = []
        for dx, dz in NEAR:
            plane = z + dz
            inside = (plane >= 0) & (plane < PLANES)
            tile = 4 * jnp.clip(plane, 0, PLANES - 1) + 2 * (xl if dx == 0 else 1 - xl) + (1 - core if other_core else core)
            value = jnp.where(inside & (mask[me, tile] > 0), 0.0, MASKED).astype(jnp.float32)
            parts.append(jnp.full((1, TILE), value, jnp.float32))
        return jnp.concatenate(parts, axis=1)

    bias_a, bias_b = bias_row(False), bias_row(True)
    width = near_a.shape[1] // 2
    half = near_a.shape[0]
    scale = HD ** (-0.5)
    for head in range(width // HD):
        cols = slice(head * HD, (head + 1) * HD)
        vcols = slice(width + head * HD, width + (head + 1) * HD)
        q = query[:, cols]
        s_a = dot(q, near_a[:, cols], NT) * scale + bias_a
        s_b = dot(q, near_b[:, cols], NT) * scale + bias_b
        top = jnp.maximum(jnp.max(s_a, axis=1, keepdims=True), jnp.max(s_b, axis=1, keepdims=True))
        e_a = jnp.exp(s_a - top)
        e_b = jnp.exp(s_b - top)
        inv = 1.0 / (jnp.sum(e_a, axis=1, keepdims=True) + jnp.sum(e_b, axis=1, keepdims=True))
        p_a = e_a * inv
        p_b = e_b * inv
        kept[head, :, :half] = p_a
        kept[head, :, half:] = p_b
        pltpu.make_async_copy(kept.at[head], probs.at[head], sent.at[head]).start()
        mixed = dot(p_a.astype(jnp.bfloat16), near_a[:, vcols]) + dot(p_b.astype(jnp.bfloat16), near_b[:, vcols])
        mixed = mixed.astype(jnp.bfloat16)
        plain[:, cols] = mixed
        turned = mixed.astype(jnp.float32).T.astype(jnp.bfloat16)
        _, copies, lines, tokens = out.shape
        start = head * HD
        while start < (head + 1) * HD:
            side, low = divmod(start, lines)
            stop = min((head + 1) * HD, (side + 1) * lines)
            piece = turned[start - head * HD : stop - head * HD]
            out[side, :, low : low + stop - start, :] = jnp.broadcast_to(piece[None], (copies,) + piece.shape)
            start = stop
    cot_out[...] = cot[...]
    for head in range(width // HD):
        pltpu.make_async_copy(kept.at[head], probs.at[head], sent.at[head]).wait()


def attend(place, mask, query, near_a, near_b, cot, copies):
    rows, width = query.shape
    heads = width // HD
    keys = 2 * near_a.shape[0]
    in_vmem = pl.BlockSpec(memory_space=VMEM)
    return pl.pallas_call(
        attend_kernel,
        out_shape=(
            jax.ShapeDtypeStruct((2, copies, width // 2, rows), jnp.bfloat16),
            jax.ShapeDtypeStruct((rows, width), jnp.bfloat16),
            pltpu.HBM((heads, rows, keys), jnp.float32),
            jax.ShapeDtypeStruct(cot.shape, cot.dtype),
        ),
        in_specs=[pl.BlockSpec(memory_space=SMEM)] * 2 + [in_vmem] * 4,
        out_specs=(in_vmem, in_vmem, pl.BlockSpec(memory_space=pltpu.HBM), in_vmem),
        scratch_shapes=[pltpu.VMEM((heads, rows, keys), jnp.float32), pltpu.SemaphoreType.DMA((heads,))],
        compiler_params=pltpu.CompilerParams(vmem_limit_bytes=16 << 20),
        cost_estimate=pl.CostEstimate(flops=4 * rows * keys * width, bytes_accessed=8 << 20, transcendentals=heads * rows * keys),
    )(place, mask, query, near_a, near_b, cot)


def up_far_kernel(place, rows_in, weight, theirs, held, arrived):
    parts, depth, width = held.shape
    rows = rows_in.shape[2]
    other = 1 - place[1]
    copies = [pltpu.make_async_copy(weight.at[part], held.at[part], arrived.at[part]) for part in range(parts)]
    for copy in copies:
        copy.start()
    total = None
    for first in range(0, parts, GROUP):
        for copy in copies[first : first + GROUP]:
            copy.wait()
        far = rows_in[pl.ds(other * parts + first, GROUP)].reshape(GROUP * depth, rows)
        term = dot(far, held[first : first + GROUP].reshape(GROUP * depth, width), TN)
        total = term if total is None else total + term
    theirs[...] = total.astype(jnp.bfloat16)


def up_far(place, rows_in, weight):
    sides, depth, rows = rows_in.shape
    parts = sides // 2
    width = weight.shape[1]
    in_vmem = pl.BlockSpec(memory_space=VMEM)
    in_hbm = pl.BlockSpec(memory_space=pltpu.HBM)
    return pl.pallas_call(
        up_far_kernel,
        out_shape=(
            jax.ShapeDtypeStruct((rows, width), jnp.bfloat16),
            VMEM((parts, depth, width), jnp.bfloat16),
        ),
        in_specs=[pl.BlockSpec(memory_space=SMEM), in_vmem, in_hbm],
        out_specs=(in_vmem,) * 2,
        scratch_shapes=[pltpu.SemaphoreType.DMA((parts,))],
        compiler_params=pltpu.CompilerParams(vmem_limit_bytes=46 << 20),
        cost_estimate=pl.CostEstimate(
            flops=2 * rows * width * parts * depth, bytes_accessed=weight.size * 2, transcendentals=0
        ),
    )(place, rows_in, weight.reshape(parts, depth, width))


def up_near_kernel(place, rows_in, held, mine):
    parts, depth, width = held.shape
    rows = rows_in.shape[2]
    near = rows_in[pl.ds(place[1] * parts, parts)].reshape(parts * depth, rows)
    mine[...] = dot(near, held[...].reshape(parts * depth, width), TN)


def up_near(place, rows_in, held):
    parts, depth, width = held.shape
    rows = rows_in.shape[2]
    in_vmem = pl.BlockSpec(memory_space=VMEM)
    return pl.pallas_call(
        up_near_kernel,
        out_shape=jax.ShapeDtypeStruct((rows, width), jnp.float32),
        in_specs=[pl.BlockSpec(memory_space=SMEM), in_vmem, in_vmem],
        out_specs=in_vmem,
        compiler_params=pltpu.CompilerParams(vmem_limit_bytes=16 << 20),
        cost_estimate=pl.CostEstimate(
            flops=2 * rows * width * parts * depth, bytes_accessed=held.size * 2, transcendentals=0
        ),
    )(place, rows_in, held)


def middle_kernel(mine, got, cot, act_out, pull_out, push_out, pair, sums):
    chunks = mine.shape[1] // 128
    power, pull = [], []
    for r in range(chunks):
        cols = slice(r * 128, (r + 1) * 128)
        v = mine[:, cols] + got[:, cols].astype(jnp.float32)
        t = jnp.tanh(ROOT * (v + CUBIC * (v * v * v)))
        act = 0.5 * v * (1.0 + t)
        slope = 0.5 * (1.0 + t) + 0.5 * v * (1.0 - t * t) * (ROOT * (1.0 + 3.0 * CUBIC * (v * v)))
        c = cot[:, cols].astype(jnp.float32)
        act_out[:, cols] = act
        pull_out[:, cols] = c * slope
        push_out[:, cols] = act * slope
        pair[0, :, cols] = (c * slope).astype(jnp.bfloat16)
        pair[1, :, cols] = (act * slope).astype(jnp.bfloat16)
        power.append(jnp.sum(act * act, axis=0, keepdims=True))
        pull.append(jnp.sum(act * c, axis=0, keepdims=True))
    lines = power + pull + [jnp.zeros((sums.shape[1] - 2 * chunks, 128), jnp.float32)]
    sums[...] = jnp.broadcast_to(jnp.concatenate(lines, axis=0).astype(jnp.bfloat16)[None], sums.shape)


def middle(mine, got, cot, copies):
    rows, width = mine.shape
    lines = -(-2 * (width // 128) // 8) * 8
    in_vmem = pl.BlockSpec(memory_space=VMEM)
    wide = jax.ShapeDtypeStruct((rows, width), jnp.float32)
    return pl.pallas_call(
        middle_kernel,
        out_shape=(
            wide,
            wide,
            wide,
            jax.ShapeDtypeStruct((2, rows, width), jnp.bfloat16),
            jax.ShapeDtypeStruct((copies, lines, 128), jnp.bfloat16),
        ),
        in_specs=[in_vmem] * 3,
        out_specs=(in_vmem,) * 5,
        compiler_params=pltpu.CompilerParams(vmem_limit_bytes=16 << 20),
        cost_estimate=pl.CostEstimate(flops=40 * rows * width, bytes_accessed=4 << 20, transcendentals=rows * width),
    )(mine, got, cot)


def down_kernel(place, act, pull, push, pair, sums, weight, out, scaled, grad):
    rows, width = act.shape
    chunks = width // 128
    own = place[1]
    total = jnp.sum(sums[...].astype(jnp.float32), axis=0)
    for r in range(chunks):
        cols = slice(r * 128, (r + 1) * 128)
        inv = lax.rsqrt(total[r : r + 1, :] * (1.0 / TOKENS) + EPSILON)
        back = total[chunks + r : chunks + r + 1, :] * -0.5 * inv * inv * inv * (2.0 / TOKENS)
        scaled[:, cols] = (act[:, cols] * inv).astype(jnp.bfloat16)
        grad[:rows, cols] = (pull[:, cols] * inv + back * push[:, cols]).astype(jnp.bfloat16)
        far = pair[0, :, cols].astype(jnp.float32) * inv + back * pair[1, :, cols].astype(jnp.float32)
        grad[rows:, cols] = far.astype(jnp.bfloat16)
    parts, depth, _ = weight.shape
    group = 4
    for first in range(0, parts, group):
        term = dot(weight[first : first + group].reshape(group * depth, width), grad[...], NT).astype(jnp.bfloat16)
        out[pl.ds(own * parts + first, group)] = term[:, :rows].reshape(group, depth, rows)
        out[pl.ds((1 - own) * parts + first, group)] = term[:, rows:].reshape(group, depth, rows)


def down(place, act, pull, push, pair, sums, weight):
    rows, width = act.shape
    parts, depth, _ = weight.shape
    in_vmem = pl.BlockSpec(memory_space=VMEM)
    return pl.pallas_call(
        down_kernel,
        out_shape=(
            jax.ShapeDtypeStruct((2 * parts, depth, rows), jnp.bfloat16),
            jax.ShapeDtypeStruct((rows, width), jnp.bfloat16),
        ),
        in_specs=[pl.BlockSpec(memory_space=SMEM)] + [in_vmem] * 6,
        out_specs=(in_vmem,) * 2,
        scratch_shapes=[pltpu.VMEM((2 * rows, width), jnp.bfloat16)],
        compiler_params=pltpu.CompilerParams(vmem_limit_bytes=16 << 20),
        cost_estimate=pl.CostEstimate(
            flops=4 * rows * width * parts * depth, bytes_accessed=weight.size * 2, transcendentals=0
        ),
    )(place, act, pull, push, pair, sums, weight)


def backward_kernel(query, near_a, near_b, attn, probs, partial, grad_query, grad_a, grad_b):
    width = query.shape[1]
    half = near_a.shape[0]
    scale = HD ** (-0.5)
    parts = partial.shape[0] // 2
    sides = []
    for side in range(2):
        total = partial[side * parts].astype(jnp.float32)
        for i in range(1, parts):
            total = total + partial[side * parts + i].astype(jnp.float32)
        sides.append(total)
    turned = jnp.concatenate(sides, axis=0)
    for head in range(width // HD):
        cols = slice(head * HD, (head + 1) * HD)
        vcols = slice(width + head * HD, width + (head + 1) * HD)
        g = turned[cols].T.astype(jnp.bfloat16)
        delta = jnp.sum(g.astype(jnp.float32) * attn[:, cols].astype(jnp.float32), axis=1, keepdims=True)
        q = query[:, cols]
        out = None
        for side, (near, result) in enumerate(((near_a, grad_a), (near_b, grad_b))):
            p = probs[head, :, side * half : (side + 1) * half]
            d = (p * (dot(g, near[:, vcols], NT) - delta)).astype(jnp.bfloat16)
            term = dot(d, near[:, cols])
            out = term if out is None else out + term
            result[:, cols] = (dot(d, q, TN) * scale).astype(jnp.bfloat16)
            result[:, vcols] = dot(p.astype(jnp.bfloat16), g, TN).astype(jnp.bfloat16)
        grad_query[:, cols] = out * scale


def backward(query, near_a, near_b, attn, probs, partial):
    rows, width = query.shape
    in_vmem = pl.BlockSpec(memory_space=VMEM)
    return pl.pallas_call(
        backward_kernel,
        out_shape=(
            jax.ShapeDtypeStruct((rows, width), jnp.float32),
            jax.ShapeDtypeStruct(near_a.shape, jnp.bfloat16),
            jax.ShapeDtypeStruct(near_b.shape, jnp.bfloat16),
        ),
        in_specs=[in_vmem] * 6,
        out_specs=(in_vmem,) * 3,
        compiler_params=pltpu.CompilerParams(vmem_limit_bytes=16 << 20),
        cost_estimate=pl.CostEstimate(
            flops=8 * rows * 2 * near_a.shape[0] * width, bytes_accessed=8 << 20, transcendentals=0
        ),
    )(query, near_a, near_b, attn, probs, partial)


def swap(value, axis):
    return lax.ppermute(value, axis, [(0, 1), (1, 0)])


def up_plane(value):
    return lax.ppermute(value, "z", [(i, (i + 1) % PLANES) for i in range(PLANES)])


def down_plane(value):
    return lax.ppermute(value, "z", [(i, (i - 1) % PLANES) for i in range(PLANES)])


def body(query, key, value, tile_mask, weight, cot):
    rows, width = query.shape
    f32, bf16 = jnp.float32, jnp.bfloat16
    place = jnp.stack([lax.axis_index("z"), lax.axis_index("xl"), lax.axis_index("core")]).astype(jnp.int32)
    half_weight = lax.all_gather(weight, ("z", "core"), axis=0, tiled=True)
    own = lax.pad(key, jnp.zeros((), bf16), ((0, 0, 0), (0, width, 0)))
    own = own + lax.pad(value, jnp.zeros((), bf16), ((0, 0, 0), (width, 0, 0)))
    from_low, from_high = up_plane(own), down_plane(own)
    own_x = swap(own, "xl")
    far_x = swap(jnp.concatenate([from_low, from_high], axis=0), "xl")
    near_a = jnp.concatenate([own, own_x, from_low, far_x[:rows], from_high, far_x[rows:]], axis=0)
    near_b = swap(near_a, "core")
    attn_out, attn, probs, cot = attend(place, tile_mask, query, near_a, near_b, cot, lax.axis_size(FSDP))
    sides, copies, depth, _ = attn_out.shape
    rows_in = lax.all_to_all(attn_out.reshape(sides * copies, depth, rows), WIDE, 0, 0)
    theirs, held = up_far(place, rows_in, half_weight)
    got = swap(theirs, "xl")
    mine = up_near(place, rows_in, held)
    act, pull, push, pair, sums = middle(mine, got, cot, lax.axis_size(SEQ))
    pair = swap(pair, "xl")
    sums = lax.all_to_all(sums, SEQ, 0, 0)
    back, scaled = down(place, act, pull, push, pair, sums, held)
    partial = lax.all_to_all(back, WIDE, 0, 0)
    grad_query, grad_a, grad_b = backward(query, near_a, near_b, attn, probs, partial)
    both = (grad_a.astype(f32) + swap(grad_b, "core").astype(f32)).reshape(3, 2, rows, 2 * width)
    to_low, to_high = both[1].astype(bf16), both[2].astype(bf16)
    here = both[0] + down_plane(to_low).astype(f32) + up_plane(to_high).astype(f32)
    grad_own = here[0] + swap(here[1].astype(bf16), "xl").astype(f32)
    return scaled, grad_query, grad_own[:, :width], grad_own[:, width:]


def solution(mesh):
    fine = Mesh(mesh.devices.reshape(PLANES, 2, 2, 4, 2), SEQ + FSDP)
    both = P(SEQ, FSDP)
    return jax.shard_map(
        body,
        mesh=fine,
        in_specs=(both, both, both, P(), both, both),
        out_specs=(both,) * 4,
        check_vma=False,
    )
```

```python
import functools

import jax
import jax.numpy as jnp
from jax import lax
from jax.experimental import pallas as pl
from jax.experimental.pallas import tpu as pltpu
from jax.sharding import Mesh, PartitionSpec as P

HD = 128
TILE = 128
TOKENS = 4096
EPSILON = 1e-05
MASKED = -1e30
ROOT = 0.7978845608028654
CUBIC = 0.044715
PLANES = 8
GROUP = 2
NEAR = ((0, 0), (1, 0), (0, -1), (1, -1), (0, 1), (1, 1))
SEQ = ("z", "xl", "core")
FSDP = ("y", "xh")
WIDE = ("xl", "y", "xh")
NT = (((1,), (1,)), ((), ()))
TN = (((0,), (0,)), ((), ()))
VMEM = pltpu.VMEM
SMEM = pltpu.SMEM


def dot(a, b, dims=(((1,), (0,)), ((), ()))):
    return lax.dot_general(a, b, dims, preferred_element_type=jnp.float32)


def attend_kernel(place, mask, query, near_a, near_b, out, plain, probs, kept, sent):
    z, xl, core = place[0], place[1], place[2]
    me = 4 * z + 2 * xl + core

    def bias_row(other_core):
        parts = []
        for dx, dz in NEAR:
            plane = z + dz
            inside = (plane >= 0) & (plane < PLANES)
            tile = 4 * jnp.clip(plane, 0, PLANES - 1) + 2 * (xl if dx == 0 else 1 - xl) + (1 - core if other_core else core)
            value = jnp.where(inside & (mask[me, tile] > 0), 0.0, MASKED).astype(jnp.float32)
            parts.append(jnp.full((1, TILE), value, jnp.float32))
        return jnp.concatenate(parts, axis=1)

    bias_a, bias_b = bias_row(False), bias_row(True)
    width = near_a.shape[1] // 2
    half = near_a.shape[0]
    scale = HD ** (-0.5)
    for head in range(width // HD):
        cols = slice(head * HD, (head + 1) * HD)
        vcols = slice(width + head * HD, width + (head + 1) * HD)
        q = query[:, cols]
        s_a = dot(q, near_a[:, cols], NT) * scale + bias_a
        s_b = dot(q, near_b[:, cols], NT) * scale + bias_b
        top = jnp.maximum(jnp.max(s_a, axis=1, keepdims=True), jnp.max(s_b, axis=1, keepdims=True))
        e_a = jnp.exp(s_a - top)
        e_b = jnp.exp(s_b - top)
        inv = 1.0 / (jnp.sum(e_a, axis=1, keepdims=True) + jnp.sum(e_b, axis=1, keepdims=True))
        p_a = (e_a * inv).astype(jnp.bfloat16)
        p_b = (e_b * inv).astype(jnp.bfloat16)
        kept[head, :, :half] = p_a
        kept[head, :, half:] = p_b
        pltpu.make_async_copy(kept.at[head], probs.at[head], sent.at[head]).start()
        mixed = dot(p_a, near_a[:, vcols]) + dot(p_b, near_b[:, vcols])
        mixed = mixed.astype(jnp.bfloat16)
        plain[:, cols] = mixed
        turned = mixed.astype(jnp.float32).T.astype(jnp.bfloat16)
        _, copies, lines, tokens = out.shape
        start = head * HD
        while start < (head + 1) * HD:
            side, low = divmod(start, lines)
            stop = min((head + 1) * HD, (side + 1) * lines)
            piece = turned[start - head * HD : stop - head * HD]
            out[side, :, low : low + stop - start, :] = jnp.broadcast_to(piece[None], (copies,) + piece.shape)
            start = stop
    for head in range(width // HD):
        pltpu.make_async_copy(kept.at[head], probs.at[head], sent.at[head]).wait()


def attend(place, mask, query, near_a, near_b, copies):
    rows, width = query.shape
    heads = width // HD
    keys = 2 * near_a.shape[0]
    in_vmem = pl.BlockSpec(memory_space=VMEM)
    return pl.pallas_call(
        attend_kernel,
        out_shape=(
            jax.ShapeDtypeStruct((2, copies, width // 2, rows), jnp.bfloat16),
            jax.ShapeDtypeStruct((rows, width), jnp.bfloat16),
            pltpu.HBM((heads, rows, keys), jnp.bfloat16),
        ),
        in_specs=[pl.BlockSpec(memory_space=SMEM)] * 2 + [in_vmem] * 3,
        out_specs=(in_vmem, in_vmem, pl.BlockSpec(memory_space=pltpu.HBM)),
        scratch_shapes=[pltpu.VMEM((heads, rows, keys), jnp.bfloat16), pltpu.SemaphoreType.DMA((heads,))],
        compiler_params=pltpu.CompilerParams(vmem_limit_bytes=16 << 20),
        cost_estimate=pl.CostEstimate(flops=4 * rows * keys * width, bytes_accessed=8 << 20, transcendentals=heads * rows * keys),
    )(place, mask, query, near_a, near_b)


def up_far_kernel(place, rows_in, weight, theirs, held, arrived):
    parts, depth, width = held.shape
    rows = rows_in.shape[2]
    other = 1 - place[1]
    copies = [pltpu.make_async_copy(weight.at[part], held.at[part], arrived.at[part]) for part in range(parts)]
    for copy in copies:
        copy.start()
    total = None
    for first in range(0, parts, GROUP):
        for copy in copies[first : first + GROUP]:
            copy.wait()
        far = rows_in[pl.ds(other * parts + first, GROUP)].reshape(GROUP * depth, rows)
        term = dot(far, held[first : first + GROUP].reshape(GROUP * depth, width), TN)
        total = term if total is None else total + term
    theirs[...] = total.astype(jnp.bfloat16)


def up_far(place, rows_in, weight):
    sides, depth, rows = rows_in.shape
    parts = sides // 2
    width = weight.shape[1]
    in_vmem = pl.BlockSpec(memory_space=VMEM)
    in_hbm = pl.BlockSpec(memory_space=pltpu.HBM)
    return pl.pallas_call(
        up_far_kernel,
        out_shape=(
            jax.ShapeDtypeStruct((rows, width), jnp.bfloat16),
            VMEM((parts, depth, width), jnp.bfloat16),
        ),
        in_specs=[pl.BlockSpec(memory_space=SMEM), in_vmem, in_hbm],
        out_specs=(in_vmem,) * 2,
        scratch_shapes=[pltpu.SemaphoreType.DMA((parts,))],
        compiler_params=pltpu.CompilerParams(vmem_limit_bytes=46 << 20),
        cost_estimate=pl.CostEstimate(
            flops=2 * rows * width * parts * depth, bytes_accessed=weight.size * 2, transcendentals=0
        ),
    )(place, rows_in, weight.reshape(parts, depth, width))


def up_near_kernel(place, rows_in, held, mine):
    parts, depth, width = held.shape
    rows = rows_in.shape[2]
    near = rows_in[pl.ds(place[1] * parts, parts)].reshape(parts * depth, rows)
    mine[...] = dot(near, held[...].reshape(parts * depth, width), TN)


def up_near(place, rows_in, held):
    parts, depth, width = held.shape
    rows = rows_in.shape[2]
    in_vmem = pl.BlockSpec(memory_space=VMEM)
    return pl.pallas_call(
        up_near_kernel,
        out_shape=jax.ShapeDtypeStruct((rows, width), jnp.float32),
        in_specs=[pl.BlockSpec(memory_space=SMEM), in_vmem, in_vmem],
        out_specs=in_vmem,
        compiler_params=pltpu.CompilerParams(vmem_limit_bytes=16 << 20),
        cost_estimate=pl.CostEstimate(
            flops=2 * rows * width * parts * depth, bytes_accessed=held.size * 2, transcendentals=0
        ),
    )(place, rows_in, held)


def middle_kernel(mine, got, cot, act_out, pull_out, push_out, pair, sums):
    chunks = mine.shape[1] // 128
    power, pull = [], []
    for r in range(chunks):
        cols = slice(r * 128, (r + 1) * 128)
        v = mine[:, cols] + got[:, cols].astype(jnp.float32)
        t = jnp.tanh(ROOT * (v + CUBIC * (v * v * v)))
        act = 0.5 * v * (1.0 + t)
        slope = 0.5 * (1.0 + t) + 0.5 * v * (1.0 - t * t) * (ROOT * (1.0 + 3.0 * CUBIC * (v * v)))
        c = cot[:, cols].astype(jnp.float32)
        act_out[:, cols] = act
        pull_out[:, cols] = c * slope
        push_out[:, cols] = act * slope
        pair[0, :, cols] = (c * slope).astype(jnp.bfloat16)
        pair[1, :, cols] = (act * slope).astype(jnp.bfloat16)
        power.append(jnp.sum(act * act, axis=0, keepdims=True))
        pull.append(jnp.sum(act * c, axis=0, keepdims=True))
    lines = power + pull + [jnp.zeros((sums.shape[1] - 2 * chunks, 128), jnp.float32)]
    sums[...] = jnp.broadcast_to(jnp.concatenate(lines, axis=0).astype(jnp.bfloat16)[None], sums.shape)


def middle(mine, got, cot, copies):
    rows, width = mine.shape
    lines = -(-2 * (width // 128) // 8) * 8
    in_vmem = pl.BlockSpec(memory_space=VMEM)
    wide = jax.ShapeDtypeStruct((rows, width), jnp.float32)
    return pl.pallas_call(
        middle_kernel,
        out_shape=(
            wide,
            wide,
            wide,
            jax.ShapeDtypeStruct((2, rows, width), jnp.bfloat16),
            jax.ShapeDtypeStruct((copies, lines, 128), jnp.bfloat16),
        ),
        in_specs=[in_vmem] * 3,
        out_specs=(in_vmem,) * 5,
        compiler_params=pltpu.CompilerParams(vmem_limit_bytes=16 << 20),
        cost_estimate=pl.CostEstimate(flops=40 * rows * width, bytes_accessed=4 << 20, transcendentals=rows * width),
    )(mine, got, cot)


def down_kernel(place, act, pull, push, pair, sums, weight, out, scaled, grad):
    rows, width = act.shape
    chunks = width // 128
    own = place[1]
    total = jnp.sum(sums[...].astype(jnp.float32), axis=0)
    for r in range(chunks):
        cols = slice(r * 128, (r + 1) * 128)
        inv = lax.rsqrt(total[r : r + 1, :] * (1.0 / TOKENS) + EPSILON)
        back = total[chunks + r : chunks + r + 1, :] * -0.5 * inv * inv * inv * (2.0 / TOKENS)
        scaled[:, cols] = (act[:, cols] * inv).astype(jnp.bfloat16)
        grad[:rows, cols] = (pull[:, cols] * inv + back * push[:, cols]).astype(jnp.bfloat16)
        far = pair[0, :, cols].astype(jnp.float32) * inv + back * pair[1, :, cols].astype(jnp.float32)
        grad[rows:, cols] = far.astype(jnp.bfloat16)
    parts, depth, _ = weight.shape
    group = 4
    for first in range(0, parts, group):
        term = dot(weight[first : first + group].reshape(group * depth, width), grad[...], NT).astype(jnp.bfloat16)
        out[pl.ds(own * parts + first, group)] = term[:, :rows].reshape(group, depth, rows)
        out[pl.ds((1 - own) * parts + first, group)] = term[:, rows:].reshape(group, depth, rows)


def down(place, act, pull, push, pair, sums, weight):
    rows, width = act.shape
    parts, depth, _ = weight.shape
    in_vmem = pl.BlockSpec(memory_space=VMEM)
    return pl.pallas_call(
        down_kernel,
        out_shape=(
            jax.ShapeDtypeStruct((2 * parts, depth, rows), jnp.bfloat16),
            jax.ShapeDtypeStruct((rows, width), jnp.bfloat16),
        ),
        in_specs=[pl.BlockSpec(memory_space=SMEM)] + [in_vmem] * 6,
        out_specs=(in_vmem,) * 2,
        scratch_shapes=[pltpu.VMEM((2 * rows, width), jnp.bfloat16)],
        compiler_params=pltpu.CompilerParams(vmem_limit_bytes=16 << 20),
        cost_estimate=pl.CostEstimate(
            flops=4 * rows * width * parts * depth, bytes_accessed=weight.size * 2, transcendentals=0
        ),
    )(place, act, pull, push, pair, sums, weight)


def backward_kernel(query, near_a, near_b, attn, probs, partial, grad_query, grad_a, grad_b):
    width = query.shape[1]
    half = near_a.shape[0]
    scale = HD ** (-0.5)
    parts = partial.shape[0] // 2
    sides = []
    for side in range(2):
        total = partial[side * parts].astype(jnp.float32)
        for i in range(1, parts):
            total = total + partial[side * parts + i].astype(jnp.float32)
        sides.append(total)
    turned = jnp.concatenate(sides, axis=0)
    for head in range(width // HD):
        cols = slice(head * HD, (head + 1) * HD)
        vcols = slice(width + head * HD, width + (head + 1) * HD)
        g = turned[cols].T.astype(jnp.bfloat16)
        delta = jnp.sum(g.astype(jnp.float32) * attn[:, cols].astype(jnp.float32), axis=1, keepdims=True)
        q = query[:, cols]
        out = None
        for side, (near, result) in enumerate(((near_a, grad_a), (near_b, grad_b))):
            p = probs[head, :, side * half : (side + 1) * half]
            d = (p.astype(jnp.float32) * (dot(g, near[:, vcols], NT) - delta)).astype(jnp.bfloat16)
            term = dot(d, near[:, cols])
            out = term if out is None else out + term
            result[:, cols] = (dot(d, q, TN) * scale).astype(jnp.bfloat16)
            result[:, vcols] = dot(p, g, TN).astype(jnp.bfloat16)
        grad_query[:, cols] = out * scale


def backward(query, near_a, near_b, attn, probs, partial):
    rows, width = query.shape
    in_vmem = pl.BlockSpec(memory_space=VMEM)
    return pl.pallas_call(
        backward_kernel,
        out_shape=(
            jax.ShapeDtypeStruct((rows, width), jnp.float32),
            jax.ShapeDtypeStruct(near_a.shape, jnp.bfloat16),
            jax.ShapeDtypeStruct(near_b.shape, jnp.bfloat16),
        ),
        in_specs=[in_vmem] * 6,
        out_specs=(in_vmem,) * 3,
        compiler_params=pltpu.CompilerParams(vmem_limit_bytes=16 << 20),
        cost_estimate=pl.CostEstimate(
            flops=8 * rows * 2 * near_a.shape[0] * width, bytes_accessed=8 << 20, transcendentals=0
        ),
    )(query, near_a, near_b, attn, probs, partial)


def swap(value, axis):
    return lax.ppermute(value, axis, [(0, 1), (1, 0)])


def up_plane(value):
    return lax.ppermute(value, "z", [(i, (i + 1) % PLANES) for i in range(PLANES)])


def down_plane(value):
    return lax.ppermute(value, "z", [(i, (i - 1) % PLANES) for i in range(PLANES)])


def shifted(value, planes, xl):
    pairs = [
        (2 * i + j, 2 * ((i + planes) % PLANES) + (j + xl) % 2) for i in range(PLANES) for j in range(2)
    ]
    return lax.ppermute(value, ("z", "xl"), pairs)


def body(query, key, value, tile_mask, weight, cot):
    rows, width = query.shape
    f32, bf16 = jnp.float32, jnp.bfloat16
    place = jnp.stack([lax.axis_index("z"), lax.axis_index("xl"), lax.axis_index("core")]).astype(jnp.int32)
    half_weight = lax.all_gather(weight, ("z", "core"), axis=0, tiled=True)
    own = lax.pad(key, jnp.zeros((), bf16), ((0, 0, 0), (0, width, 0)))
    own = own + lax.pad(value, jnp.zeros((), bf16), ((0, 0, 0), (width, 0, 0)))
    from_low, from_high = up_plane(own), down_plane(own)
    own_x = swap(own, "xl")
    far_x = swap(jnp.concatenate([from_low, from_high], axis=0), "xl")
    near_a = jnp.concatenate([own, own_x, from_low, far_x[:rows], from_high, far_x[rows:]], axis=0)
    near_b = swap(near_a, "core")
    attn_out, attn, probs = attend(place, tile_mask, query, near_a, near_b, lax.axis_size(FSDP))
    sides, copies, depth, _ = attn_out.shape
    rows_in = lax.all_to_all(attn_out.reshape(sides * copies, depth, rows), WIDE, 0, 0)
    theirs, held = up_far(place, rows_in, half_weight)
    got = swap(theirs, "xl")
    mine = up_near(place, rows_in, held)
    act, pull, push, pair, sums = middle(mine, got, cot, lax.axis_size(SEQ))
    pair = swap(pair, "xl")
    sums = lax.all_to_all(sums, SEQ, 0, 0)
    back, scaled = down(place, act, pull, push, pair, sums, held)
    partial = lax.all_to_all(back, WIDE, 0, 0)
    grad_query, grad_a, grad_b = backward(query, near_a, near_b, attn, probs, partial)
    both = grad_a.astype(f32) + swap(grad_b, "core").astype(f32)
    blocks = [both[i * rows : (i + 1) * rows] for i in range(6)]
    moves = ((1, 0, 1), (3, -1, 1), (5, 1, 1), (2, -1, 0), (4, 1, 0))
    arrived = [shifted(blocks[i].astype(bf16), planes, xl) for i, planes, xl in moves]
    grad_own = blocks[0]
    for block in arrived:
        grad_own = grad_own + block.astype(f32)
    return scaled, grad_query, grad_own[:, :width], grad_own[:, width:]


def solution(mesh):
    fine = Mesh(mesh.devices.reshape(PLANES, 2, 2, 4, 2), SEQ + FSDP)
    both = P(SEQ, FSDP)
    return jax.shard_map(
        body,
        mesh=fine,
        in_specs=(both, both, both, P(), both, both),
        out_specs=(both,) * 4,
        check_vma=False,
    )
```

```python
import functools

import jax
import jax.numpy as jnp
from jax import lax
from jax.experimental import pallas as pl
from jax.experimental.pallas import tpu as pltpu
from jax.sharding import Mesh, PartitionSpec as P

HD = 128
TILE = 128
TOKENS = 4096
EPSILON = 1e-05
MASKED = -1e30
ROOT = 0.7978845608028654
CUBIC = 0.044715
PLANES = 8
GROUP = 2
NEAR = ((0, 0), (1, 0), (0, -1), (1, -1), (0, 1), (1, 1))
SEQ = ("z", "xl", "core")
FSDP = ("y", "xh")
WIDE = ("xl", "y", "xh")
NT = (((1,), (1,)), ((), ()))
TN = (((0,), (0,)), ((), ()))
VMEM = pltpu.VMEM
SMEM = pltpu.SMEM


def dot(a, b, dims=(((1,), (0,)), ((), ()))):
    return lax.dot_general(a, b, dims, preferred_element_type=jnp.float32)


def attend_kernel(place, mask, query, near_a, near_b, out, plain, probs, kept, sent):
    z, xl, core = place[0], place[1], place[2]
    me = 4 * z + 2 * xl + core

    def bias_row(other_core):
        parts = []
        for dx, dz in NEAR:
            plane = z + dz
            inside = (plane >= 0) & (plane < PLANES)
            tile = 4 * jnp.clip(plane, 0, PLANES - 1) + 2 * (xl if dx == 0 else 1 - xl) + (1 - core if other_core else core)
            value = jnp.where(inside & (mask[me, tile] > 0), 0.0, MASKED).astype(jnp.float32)
            parts.append(jnp.full((1, TILE), value, jnp.float32))
        return jnp.concatenate(parts, axis=1)

    bias_a, bias_b = bias_row(False), bias_row(True)
    width = near_a.shape[1] // 2
    half = near_a.shape[0]
    scale = HD ** (-0.5)
    for head in range(width // HD):
        cols = slice(head * HD, (head + 1) * HD)
        vcols = slice(width + head * HD, width + (head + 1) * HD)
        q = query[:, cols]
        s_a = dot(q, near_a[:, cols], NT) * scale + bias_a
        s_b = dot(q, near_b[:, cols], NT) * scale + bias_b
        top = jnp.maximum(jnp.max(s_a, axis=1, keepdims=True), jnp.max(s_b, axis=1, keepdims=True))
        e_a = jnp.exp(s_a - top)
        e_b = jnp.exp(s_b - top)
        inv = 1.0 / (jnp.sum(e_a, axis=1, keepdims=True) + jnp.sum(e_b, axis=1, keepdims=True))
        p_a = (e_a * inv).astype(jnp.bfloat16)
        p_b = (e_b * inv).astype(jnp.bfloat16)
        kept[head, :, :half] = p_a
        kept[head, :, half:] = p_b
        pltpu.make_async_copy(kept.at[head], probs.at[head], sent.at[head]).start()
        mixed = dot(p_a, near_a[:, vcols]) + dot(p_b, near_b[:, vcols])
        mixed = mixed.astype(jnp.bfloat16)
        plain[:, cols] = mixed
        turned = mixed.astype(jnp.float32).T.astype(jnp.bfloat16)
        _, copies, lines, tokens = out.shape
        start = head * HD
        while start < (head + 1) * HD:
            side, low = divmod(start, lines)
            stop = min((head + 1) * HD, (side + 1) * lines)
            piece = turned[start - head * HD : stop - head * HD]
            out[side, :, low : low + stop - start, :] = jnp.broadcast_to(piece[None], (copies,) + piece.shape)
            start = stop
    for head in range(width // HD):
        pltpu.make_async_copy(kept.at[head], probs.at[head], sent.at[head]).wait()


def attend(place, mask, query, near_a, near_b, copies):
    rows, width = query.shape
    heads = width // HD
    keys = 2 * near_a.shape[0]
    in_vmem = pl.BlockSpec(memory_space=VMEM)
    return pl.pallas_call(
        attend_kernel,
        out_shape=(
            jax.ShapeDtypeStruct((2, copies, width // 2, rows), jnp.bfloat16),
            jax.ShapeDtypeStruct((rows, width), jnp.bfloat16),
            pltpu.HBM((heads, rows, keys), jnp.bfloat16),
        ),
        in_specs=[pl.BlockSpec(memory_space=SMEM)] * 2 + [in_vmem] * 3,
        out_specs=(in_vmem, in_vmem, pl.BlockSpec(memory_space=pltpu.HBM)),
        scratch_shapes=[pltpu.VMEM((heads, rows, keys), jnp.bfloat16), pltpu.SemaphoreType.DMA((heads,))],
        compiler_params=pltpu.CompilerParams(vmem_limit_bytes=16 << 20),
        cost_estimate=pl.CostEstimate(flops=4 * rows * keys * width, bytes_accessed=8 << 20, transcendentals=heads * rows * keys),
    )(place, mask, query, near_a, near_b)


def up_far_kernel(place, rows_in, weight, theirs, held, arrived):
    parts, depth, width = held.shape
    rows = rows_in.shape[2]
    other = 1 - place[1]
    copies = [pltpu.make_async_copy(weight.at[part], held.at[part], arrived.at[part]) for part in range(parts)]
    for copy in copies:
        copy.start()
    total = None
    for first in range(0, parts, GROUP):
        for copy in copies[first : first + GROUP]:
            copy.wait()
        far = rows_in[pl.ds(other * parts + first, GROUP)].reshape(GROUP * depth, rows)
        term = dot(far, held[first : first + GROUP].reshape(GROUP * depth, width), TN)
        total = term if total is None else total + term
    theirs[...] = total.astype(jnp.bfloat16)


def up_far(place, rows_in, weight):
    sides, depth, rows = rows_in.shape
    parts = sides // 2
    width = weight.shape[1]
    in_vmem = pl.BlockSpec(memory_space=VMEM)
    in_hbm = pl.BlockSpec(memory_space=pltpu.HBM)
    return pl.pallas_call(
        up_far_kernel,
        out_shape=(
            jax.ShapeDtypeStruct((rows, width), jnp.bfloat16),
            VMEM((parts, depth, width), jnp.bfloat16),
        ),
        in_specs=[pl.BlockSpec(memory_space=SMEM), in_vmem, in_hbm],
        out_specs=(in_vmem,) * 2,
        scratch_shapes=[pltpu.SemaphoreType.DMA((parts,))],
        compiler_params=pltpu.CompilerParams(vmem_limit_bytes=46 << 20),
        cost_estimate=pl.CostEstimate(
            flops=2 * rows * width * parts * depth, bytes_accessed=weight.size * 2, transcendentals=0
        ),
    )(place, rows_in, weight.reshape(parts, depth, width))


def up_near_kernel(place, rows_in, held, mine):
    parts, depth, width = held.shape
    rows = rows_in.shape[2]
    near = rows_in[pl.ds(place[1] * parts, parts)].reshape(parts * depth, rows)
    mine[...] = dot(near, held[...].reshape(parts * depth, width), TN)


def up_near(place, rows_in, held):
    parts, depth, width = held.shape
    rows = rows_in.shape[2]
    in_vmem = pl.BlockSpec(memory_space=VMEM)
    return pl.pallas_call(
        up_near_kernel,
        out_shape=jax.ShapeDtypeStruct((rows, width), jnp.float32),
        in_specs=[pl.BlockSpec(memory_space=SMEM), in_vmem, in_vmem],
        out_specs=in_vmem,
        compiler_params=pltpu.CompilerParams(vmem_limit_bytes=16 << 20),
        cost_estimate=pl.CostEstimate(
            flops=2 * rows * width * parts * depth, bytes_accessed=held.size * 2, transcendentals=0
        ),
    )(place, rows_in, held)


def middle_kernel(mine, got, cot, act_out, pull_out, push_out, pair, sums):
    chunks = mine.shape[1] // 128
    power, pull = [], []
    for r in range(chunks):
        cols = slice(r * 128, (r + 1) * 128)
        v = mine[:, cols] + got[:, cols].astype(jnp.float32)
        t = jnp.tanh(ROOT * (v + CUBIC * (v * v * v)))
        act = 0.5 * v * (1.0 + t)
        slope = 0.5 * (1.0 + t) + 0.5 * v * (1.0 - t * t) * (ROOT * (1.0 + 3.0 * CUBIC * (v * v)))
        c = cot[:, cols].astype(jnp.float32)
        act_out[:, cols] = act
        pull_out[:, cols] = c * slope
        push_out[:, cols] = act * slope
        pair[0, :, cols] = (c * slope).astype(jnp.bfloat16)
        pair[1, :, cols] = (act * slope).astype(jnp.bfloat16)
        power.append(jnp.sum(act * act, axis=0, keepdims=True))
        pull.append(jnp.sum(act * c, axis=0, keepdims=True))
    lines = power + pull + [jnp.zeros((sums.shape[1] - 2 * chunks, 128), jnp.float32)]
    sums[...] = jnp.broadcast_to(jnp.concatenate(lines, axis=0).astype(jnp.bfloat16)[None], sums.shape)


def middle(mine, got, cot, copies):
    rows, width = mine.shape
    lines = -(-2 * (width // 128) // 8) * 8
    in_vmem = pl.BlockSpec(memory_space=VMEM)
    wide = jax.ShapeDtypeStruct((rows, width), jnp.float32)
    return pl.pallas_call(
        middle_kernel,
        out_shape=(
            wide,
            wide,
            wide,
            jax.ShapeDtypeStruct((2, rows, width), jnp.bfloat16),
            jax.ShapeDtypeStruct((copies, lines, 128), jnp.bfloat16),
        ),
        in_specs=[in_vmem] * 3,
        out_specs=(in_vmem,) * 5,
        compiler_params=pltpu.CompilerParams(vmem_limit_bytes=16 << 20),
        cost_estimate=pl.CostEstimate(flops=40 * rows * width, bytes_accessed=4 << 20, transcendentals=rows * width),
    )(mine, got, cot)


def down_kernel(place, act, pull, push, pair, sums, weight, out, scaled, grad):
    rows, width = act.shape
    chunks = width // 128
    own = place[1]
    total = jnp.sum(sums[...].astype(jnp.float32), axis=0)
    for r in range(chunks):
        cols = slice(r * 128, (r + 1) * 128)
        inv = lax.rsqrt(total[r : r + 1, :] * (1.0 / TOKENS) + EPSILON)
        back = total[chunks + r : chunks + r + 1, :] * -0.5 * inv * inv * inv * (2.0 / TOKENS)
        scaled[:, cols] = (act[:, cols] * inv).astype(jnp.bfloat16)
        grad[:rows, cols] = (pull[:, cols] * inv + back * push[:, cols]).astype(jnp.bfloat16)
        far = pair[0, :, cols].astype(jnp.float32) * inv + back * pair[1, :, cols].astype(jnp.float32)
        grad[rows:, cols] = far.astype(jnp.bfloat16)
    parts, depth, _ = weight.shape
    group = 4
    for first in range(0, parts, group):
        term = dot(weight[first : first + group].reshape(group * depth, width), grad[...], NT).astype(jnp.bfloat16)
        out[pl.ds(own * parts + first, group)] = term[:, :rows].reshape(group, depth, rows)
        out[pl.ds((1 - own) * parts + first, group)] = term[:, rows:].reshape(group, depth, rows)


def down(place, act, pull, push, pair, sums, weight):
    rows, width = act.shape
    parts, depth, _ = weight.shape
    in_vmem = pl.BlockSpec(memory_space=VMEM)
    return pl.pallas_call(
        down_kernel,
        out_shape=(
            jax.ShapeDtypeStruct((2 * parts, depth, rows), jnp.bfloat16),
            jax.ShapeDtypeStruct((rows, width), jnp.bfloat16),
        ),
        in_specs=[pl.BlockSpec(memory_space=SMEM)] + [in_vmem] * 6,
        out_specs=(in_vmem,) * 2,
        scratch_shapes=[pltpu.VMEM((2 * rows, width), jnp.bfloat16)],
        compiler_params=pltpu.CompilerParams(vmem_limit_bytes=16 << 20),
        cost_estimate=pl.CostEstimate(
            flops=4 * rows * width * parts * depth, bytes_accessed=weight.size * 2, transcendentals=0
        ),
    )(place, act, pull, push, pair, sums, weight)


def backward_kernel(side, query, near, attn, probs, *refs):
    if side == 1:
        partial, grad_query, result, kept = refs
        parts = partial.shape[0] // 2
        halves = []
        for x in range(2):
            total = partial[x * parts].astype(jnp.float32)
            for i in range(1, parts):
                total = total + partial[x * parts + i].astype(jnp.float32)
            halves.append(total)
        turned = jnp.concatenate(halves, axis=0)
    else:
        kept, before, grad_query, result = refs
    width = query.shape[1]
    half = near.shape[0]
    scale = HD ** (-0.5)
    for head in range(width // HD):
        cols = slice(head * HD, (head + 1) * HD)
        vcols = slice(width + head * HD, width + (head + 1) * HD)
        if side == 1:
            g = turned[cols].T.astype(jnp.bfloat16)
            kept[:, cols] = g
        else:
            g = kept[:, cols]
        delta = jnp.sum(g.astype(jnp.float32) * attn[:, cols].astype(jnp.float32), axis=1, keepdims=True)
        p = probs[head, :, side * half : (side + 1) * half]
        d = (p.astype(jnp.float32) * (dot(g, near[:, vcols], NT) - delta)).astype(jnp.bfloat16)
        result[:, cols] = (dot(d, query[:, cols], TN) * scale).astype(jnp.bfloat16)
        result[:, vcols] = dot(p, g, TN).astype(jnp.bfloat16)
        term = dot(d, near[:, cols]) * scale
        grad_query[:, cols] = term if side == 1 else before[:, cols] + term


def backward(side, query, near, attn, probs, *rest):
    rows, width = query.shape
    in_vmem = pl.BlockSpec(memory_space=VMEM)
    shapes = [
        jax.ShapeDtypeStruct((rows, width), jnp.float32),
        jax.ShapeDtypeStruct(near.shape, jnp.bfloat16),
    ]
    if side == 1:
        shapes.append(jax.ShapeDtypeStruct((rows, width), jnp.bfloat16))
    return pl.pallas_call(
        functools.partial(backward_kernel, side),
        out_shape=tuple(shapes),
        in_specs=[in_vmem] * (4 + len(rest)),
        out_specs=(in_vmem,) * len(shapes),
        compiler_params=pltpu.CompilerParams(vmem_limit_bytes=16 << 20),
        cost_estimate=pl.CostEstimate(
            flops=8 * rows * near.shape[0] * width, bytes_accessed=4 << 20, transcendentals=0
        ),
    )(query, near, attn, probs, *rest)


def swap(value, axis):
    return lax.ppermute(value, axis, [(0, 1), (1, 0)])


def up_plane(value):
    return lax.ppermute(value, "z", [(i, (i + 1) % PLANES) for i in range(PLANES)])


def down_plane(value):
    return lax.ppermute(value, "z", [(i, (i - 1) % PLANES) for i in range(PLANES)])


def shifted(value, planes, xl):
    pairs = [
        (2 * i + j, 2 * ((i + planes) % PLANES) + (j + xl) % 2) for i in range(PLANES) for j in range(2)
    ]
    return lax.ppermute(value, ("z", "xl"), pairs)


def body(query, key, value, tile_mask, weight, cot):
    rows, width = query.shape
    f32, bf16 = jnp.float32, jnp.bfloat16
    place = jnp.stack([lax.axis_index("z"), lax.axis_index("xl"), lax.axis_index("core")]).astype(jnp.int32)
    half_weight = lax.all_gather(weight, ("z", "core"), axis=0, tiled=True)
    own = lax.pad(key, jnp.zeros((), bf16), ((0, 0, 0), (0, width, 0)))
    own = own + lax.pad(value, jnp.zeros((), bf16), ((0, 0, 0), (width, 0, 0)))
    from_low, from_high = up_plane(own), down_plane(own)
    own_x = swap(own, "xl")
    far_x = swap(jnp.concatenate([from_low, from_high], axis=0), "xl")
    near_a = jnp.concatenate([own, own_x, from_low, far_x[:rows], from_high, far_x[rows:]], axis=0)
    near_b = swap(near_a, "core")
    attn_out, attn, probs = attend(place, tile_mask, query, near_a, near_b, lax.axis_size(FSDP))
    sides, copies, depth, _ = attn_out.shape
    rows_in = lax.all_to_all(attn_out.reshape(sides * copies, depth, rows), WIDE, 0, 0)
    theirs, held = up_far(place, rows_in, half_weight)
    got = swap(theirs, "xl")
    mine = up_near(place, rows_in, held)
    act, pull, push, pair, sums = middle(mine, got, cot, lax.axis_size(SEQ))
    pair = swap(pair, "xl")
    sums = lax.all_to_all(sums, SEQ, 0, 0)
    back, scaled = down(place, act, pull, push, pair, sums, held)
    partial = lax.all_to_all(back, WIDE, 0, 0)
    grad_query, grad_b, grad = backward(1, query, near_b, attn, probs, partial)
    grad_b = swap(grad_b, "core")
    grad_query, grad_a = backward(0, query, near_a, attn, probs, grad, grad_query)
    blocks = [
        grad_a[i * rows : (i + 1) * rows].astype(f32) + grad_b[i * rows : (i + 1) * rows].astype(f32) for i in range(6)
    ]
    moves = ((3, -1, 1), (5, 1, 1), (2, -1, 0), (4, 1, 0), (1, 0, 1))
    arrived = [shifted(blocks[i].astype(bf16), planes, xl) for i, planes, xl in moves]
    terms = [blocks[0]] + [block.astype(f32) for block in arrived]
    grad_key = functools.reduce(jnp.add, [term[:, :width] for term in terms])
    grad_value = functools.reduce(jnp.add, [term[:, width:] for term in terms])
    return scaled, grad_query, grad_key, grad_value


def solution(mesh):
    fine = Mesh(mesh.devices.reshape(PLANES, 2, 2, 4, 2), SEQ + FSDP)
    both = P(SEQ, FSDP)
    return jax.shard_map(
        body,
        mesh=fine,
        in_specs=(both, both, both, P(), both, both),
        out_specs=(both,) * 4,
        check_vma=False,
    )
```

```python
import functools

import jax
import jax.numpy as jnp
from jax import lax
from jax.experimental import pallas as pl
from jax.experimental.pallas import tpu as pltpu
from jax.sharding import Mesh, PartitionSpec as P

HD = 128
TILE = 128
TOKENS = 4096
EPSILON = 1e-05
MASKED = -1e30
ROOT = 0.7978845608028654
CUBIC = 0.044715
PLANES = 8
GROUP = 2
NEAR = ((0, 0), (1, 0), (0, -1), (1, -1), (0, 1), (1, 1))
SEQ = ("z", "xl", "core")
FSDP = ("y", "xh")
WIDE = ("xl", "y", "xh")
NT = (((1,), (1,)), ((), ()))
TN = (((0,), (0,)), ((), ()))
VMEM = pltpu.VMEM
SMEM = pltpu.SMEM


def dot(a, b, dims=(((1,), (0,)), ((), ()))):
    return lax.dot_general(a, b, dims, preferred_element_type=jnp.float32)


def attend_kernel(place, mask, query, near_a, near_b, out, plain, probs, kept, sent):
    z, xl, core = place[0], place[1], place[2]
    me = 4 * z + 2 * xl + core

    def bias_row(other_core):
        parts = []
        for dx, dz in NEAR:
            plane = z + dz
            inside = (plane >= 0) & (plane < PLANES)
            tile = 4 * jnp.clip(plane, 0, PLANES - 1) + 2 * (xl if dx == 0 else 1 - xl) + (1 - core if other_core else core)
            value = jnp.where(inside & (mask[me, tile] > 0), 0.0, MASKED).astype(jnp.float32)
            parts.append(jnp.full((1, TILE), value, jnp.float32))
        return jnp.concatenate(parts, axis=1)

    bias_a, bias_b = bias_row(False), bias_row(True)
    width = near_a.shape[1] // 2
    half = near_a.shape[0]
    scale = HD ** (-0.5)
    for head in range(width // HD):
        cols = slice(head * HD, (head + 1) * HD)
        vcols = slice(width + head * HD, width + (head + 1) * HD)
        q = query[:, cols]
        s_a = dot(q, near_a[:, cols], NT) * scale + bias_a
        s_b = dot(q, near_b[:, cols], NT) * scale + bias_b
        top = jnp.maximum(jnp.max(s_a, axis=1, keepdims=True), jnp.max(s_b, axis=1, keepdims=True))
        e_a = jnp.exp(s_a - top)
        e_b = jnp.exp(s_b - top)
        inv = 1.0 / (jnp.sum(e_a, axis=1, keepdims=True) + jnp.sum(e_b, axis=1, keepdims=True))
        p_a = (e_a * inv).astype(jnp.bfloat16)
        p_b = (e_b * inv).astype(jnp.bfloat16)
        kept[head, :, :half] = p_a
        kept[head, :, half:] = p_b
        pltpu.make_async_copy(kept.at[head], probs.at[head], sent.at[head]).start()
        mixed = dot(p_a, near_a[:, vcols]) + dot(p_b, near_b[:, vcols])
        mixed = mixed.astype(jnp.bfloat16)
        plain[:, cols] = mixed
        turned = mixed.astype(jnp.float32).T.astype(jnp.bfloat16)
        _, copies, lines, tokens = out.shape
        start = head * HD
        while start < (head + 1) * HD:
            side, low = divmod(start, lines)
            stop = min((head + 1) * HD, (side + 1) * lines)
            piece = turned[start - head * HD : stop - head * HD]
            out[side, :, low : low + stop - start, :] = jnp.broadcast_to(piece[None], (copies,) + piece.shape)
            start = stop
    for head in range(width // HD):
        pltpu.make_async_copy(kept.at[head], probs.at[head], sent.at[head]).wait()


def attend(place, mask, query, near_a, near_b, copies):
    rows, width = query.shape
    heads = width // HD
    keys = 2 * near_a.shape[0]
    in_vmem = pl.BlockSpec(memory_space=VMEM)
    return pl.pallas_call(
        attend_kernel,
        out_shape=(
            jax.ShapeDtypeStruct((2, copies, width // 2, rows), jnp.bfloat16),
            jax.ShapeDtypeStruct((rows, width), jnp.bfloat16),
            pltpu.HBM((heads, rows, keys), jnp.bfloat16),
        ),
        in_specs=[pl.BlockSpec(memory_space=SMEM)] * 2 + [in_vmem] * 3,
        out_specs=(in_vmem, in_vmem, pl.BlockSpec(memory_space=pltpu.HBM)),
        scratch_shapes=[pltpu.VMEM((heads, rows, keys), jnp.bfloat16), pltpu.SemaphoreType.DMA((heads,))],
        compiler_params=pltpu.CompilerParams(vmem_limit_bytes=16 << 20),
        cost_estimate=pl.CostEstimate(flops=4 * rows * keys * width, bytes_accessed=8 << 20, transcendentals=heads * rows * keys),
    )(place, mask, query, near_a, near_b)


def up_far_kernel(place, rows_in, weight, theirs, held, arrived):
    parts, depth, width = held.shape
    rows = rows_in.shape[2]
    other = 1 - place[1]
    copies = [pltpu.make_async_copy(weight.at[part], held.at[part], arrived.at[part]) for part in range(parts)]
    for copy in copies:
        copy.start()
    total = None
    for first in range(0, parts, GROUP):
        for copy in copies[first : first + GROUP]:
            copy.wait()
        far = rows_in[pl.ds(other * parts + first, GROUP)].reshape(GROUP * depth, rows)
        term = dot(far, held[first : first + GROUP].reshape(GROUP * depth, width), TN)
        total = term if total is None else total + term
    theirs[...] = total.astype(jnp.bfloat16)


def up_far(place, rows_in, weight):
    sides, depth, rows = rows_in.shape
    parts = sides // 2
    width = weight.shape[1]
    in_vmem = pl.BlockSpec(memory_space=VMEM)
    in_hbm = pl.BlockSpec(memory_space=pltpu.HBM)
    return pl.pallas_call(
        up_far_kernel,
        out_shape=(
            jax.ShapeDtypeStruct((rows, width), jnp.bfloat16),
            VMEM((parts, depth, width), jnp.bfloat16),
        ),
        in_specs=[pl.BlockSpec(memory_space=SMEM), in_vmem, in_hbm],
        out_specs=(in_vmem,) * 2,
        scratch_shapes=[pltpu.SemaphoreType.DMA((parts,))],
        compiler_params=pltpu.CompilerParams(vmem_limit_bytes=46 << 20),
        cost_estimate=pl.CostEstimate(
            flops=2 * rows * width * parts * depth, bytes_accessed=weight.size * 2, transcendentals=0
        ),
    )(place, rows_in, weight.reshape(parts, depth, width))


def up_near_kernel(place, rows_in, held, mine):
    parts, depth, width = held.shape
    rows = rows_in.shape[2]
    near = rows_in[pl.ds(place[1] * parts, parts)].reshape(parts * depth, rows)
    mine[...] = dot(near, held[...].reshape(parts * depth, width), TN)


def up_near(place, rows_in, held):
    parts, depth, width = held.shape
    rows = rows_in.shape[2]
    in_vmem = pl.BlockSpec(memory_space=VMEM)
    return pl.pallas_call(
        up_near_kernel,
        out_shape=jax.ShapeDtypeStruct((rows, width), jnp.float32),
        in_specs=[pl.BlockSpec(memory_space=SMEM), in_vmem, in_vmem],
        out_specs=in_vmem,
        compiler_params=pltpu.CompilerParams(vmem_limit_bytes=16 << 20),
        cost_estimate=pl.CostEstimate(
            flops=2 * rows * width * parts * depth, bytes_accessed=held.size * 2, transcendentals=0
        ),
    )(place, rows_in, held)


def middle_kernel(mine, got, cot, act_out, pull_out, push_out, pair, sums):
    chunks = mine.shape[1] // 128
    power, pull = [], []
    for r in range(chunks):
        cols = slice(r * 128, (r + 1) * 128)
        v = mine[:, cols] + got[:, cols].astype(jnp.float32)
        t = jnp.tanh(ROOT * (v + CUBIC * (v * v * v)))
        act = 0.5 * v * (1.0 + t)
        slope = 0.5 * (1.0 + t) + 0.5 * v * (1.0 - t * t) * (ROOT * (1.0 + 3.0 * CUBIC * (v * v)))
        c = cot[:, cols].astype(jnp.float32)
        act_out[:, cols] = act
        pull_out[:, cols] = c * slope
        push_out[:, cols] = act * slope
        pair[0, :, cols] = (c * slope).astype(jnp.bfloat16)
        pair[1, :, cols] = (act * slope).astype(jnp.bfloat16)
        power.append(jnp.sum(act * act, axis=0, keepdims=True))
        pull.append(jnp.sum(act * c, axis=0, keepdims=True))
    lines = power + pull + [jnp.zeros((sums.shape[1] - 2 * chunks, 128), jnp.float32)]
    sums[...] = jnp.broadcast_to(jnp.concatenate(lines, axis=0).astype(jnp.bfloat16)[None], sums.shape)


def middle(mine, got, cot, copies):
    rows, width = mine.shape
    lines = -(-2 * (width // 128) // 8) * 8
    in_vmem = pl.BlockSpec(memory_space=VMEM)
    wide = jax.ShapeDtypeStruct((rows, width), jnp.float32)
    return pl.pallas_call(
        middle_kernel,
        out_shape=(
            wide,
            wide,
            wide,
            jax.ShapeDtypeStruct((2, rows, width), jnp.bfloat16),
            jax.ShapeDtypeStruct((copies, lines, 128), jnp.bfloat16),
        ),
        in_specs=[in_vmem] * 3,
        out_specs=(in_vmem,) * 5,
        compiler_params=pltpu.CompilerParams(vmem_limit_bytes=16 << 20),
        cost_estimate=pl.CostEstimate(flops=40 * rows * width, bytes_accessed=4 << 20, transcendentals=rows * width),
    )(mine, got, cot)


def down_kernel(place, pull, push, pair, sums, weight, out, scales, grad):
    rows, width = pull.shape
    chunks = width // 128
    own = place[1]
    total = jnp.sum(sums[...].astype(jnp.float32), axis=0)
    for r in range(chunks):
        cols = slice(r * 128, (r + 1) * 128)
        inv = lax.rsqrt(total[r : r + 1, :] * (1.0 / TOKENS) + EPSILON)
        back = total[chunks + r : chunks + r + 1, :] * -0.5 * inv * inv * inv * (2.0 / TOKENS)
        scales[r : r + 1, :] = inv
        grad[:rows, cols] = (pull[:, cols] * inv + back * push[:, cols]).astype(jnp.bfloat16)
        far = pair[0, :, cols].astype(jnp.float32) * inv + back * pair[1, :, cols].astype(jnp.float32)
        grad[rows:, cols] = far.astype(jnp.bfloat16)
    parts, depth, _ = weight.shape
    group = 4
    for first in range(0, parts, group):
        term = dot(weight[first : first + group].reshape(group * depth, width), grad[...], NT).astype(jnp.bfloat16)
        out[pl.ds(own * parts + first, group)] = term[:, :rows].reshape(group, depth, rows)
        out[pl.ds((1 - own) * parts + first, group)] = term[:, rows:].reshape(group, depth, rows)


def down(place, pull, push, pair, sums, weight):
    rows, width = pull.shape
    parts, depth, _ = weight.shape
    in_vmem = pl.BlockSpec(memory_space=VMEM)
    return pl.pallas_call(
        down_kernel,
        out_shape=(
            jax.ShapeDtypeStruct((2 * parts, depth, rows), jnp.bfloat16),
            jax.ShapeDtypeStruct((-(-(width // 128) // 8) * 8, 128), jnp.float32),
        ),
        in_specs=[pl.BlockSpec(memory_space=SMEM)] + [in_vmem] * 5,
        out_specs=(in_vmem,) * 2,
        scratch_shapes=[pltpu.VMEM((2 * rows, width), jnp.bfloat16)],
        compiler_params=pltpu.CompilerParams(vmem_limit_bytes=16 << 20),
        cost_estimate=pl.CostEstimate(
            flops=4 * rows * width * parts * depth, bytes_accessed=weight.size * 2, transcendentals=0
        ),
    )(place, pull, push, pair, sums, weight)


def scale_kernel(act, scales, scaled):
    for r in range(act.shape[1] // 128):
        cols = slice(r * 128, (r + 1) * 128)
        scaled[:, cols] = (act[:, cols] * scales[r : r + 1, :]).astype(jnp.bfloat16)


def scale(act, scales):
    in_vmem = pl.BlockSpec(memory_space=VMEM)
    return pl.pallas_call(
        scale_kernel,
        out_shape=jax.ShapeDtypeStruct(act.shape, jnp.bfloat16),
        in_specs=[in_vmem] * 2,
        out_specs=in_vmem,
        compiler_params=pltpu.CompilerParams(vmem_limit_bytes=16 << 20),
        cost_estimate=pl.CostEstimate(flops=act.size, bytes_accessed=6 * act.size, transcendentals=0),
    )(act, scales)


def backward_kernel(side, query, near, attn, probs, *refs):
    if side == 1:
        partial, grad_query, result, kept = refs
        parts = partial.shape[0] // 2
        halves = []
        for x in range(2):
            total = partial[x * parts].astype(jnp.float32)
            for i in range(1, parts):
                total = total + partial[x * parts + i].astype(jnp.float32)
            halves.append(total)
        turned = jnp.concatenate(halves, axis=0)
    else:
        kept, before, grad_query, result = refs
    width = query.shape[1]
    half = near.shape[0]
    scale = HD ** (-0.5)
    for head in range(width // HD):
        cols = slice(head * HD, (head + 1) * HD)
        vcols = slice(width + head * HD, width + (head + 1) * HD)
        if side == 1:
            g = turned[cols].T.astype(jnp.bfloat16)
            kept[:, cols] = g
        else:
            g = kept[:, cols]
        delta = jnp.sum(g.astype(jnp.float32) * attn[:, cols].astype(jnp.float32), axis=1, keepdims=True)
        p = probs[head, :, side * half : (side + 1) * half]
        d = (p.astype(jnp.float32) * (dot(g, near[:, vcols], NT) - delta)).astype(jnp.bfloat16)
        result[:, cols] = (dot(d, query[:, cols], TN) * scale).astype(jnp.bfloat16)
        result[:, vcols] = dot(p, g, TN).astype(jnp.bfloat16)
        term = dot(d, near[:, cols]) * scale
        grad_query[:, cols] = term if side == 1 else before[:, cols] + term


def backward(side, query, near, attn, probs, *rest):
    rows, width = query.shape
    in_vmem = pl.BlockSpec(memory_space=VMEM)
    shapes = [
        jax.ShapeDtypeStruct((rows, width), jnp.float32),
        jax.ShapeDtypeStruct(near.shape, jnp.bfloat16),
    ]
    if side == 1:
        shapes.append(jax.ShapeDtypeStruct((rows, width), jnp.bfloat16))
    return pl.pallas_call(
        functools.partial(backward_kernel, side),
        out_shape=tuple(shapes),
        in_specs=[in_vmem] * (4 + len(rest)),
        out_specs=(in_vmem,) * len(shapes),
        compiler_params=pltpu.CompilerParams(vmem_limit_bytes=16 << 20),
        cost_estimate=pl.CostEstimate(
            flops=8 * rows * near.shape[0] * width, bytes_accessed=4 << 20, transcendentals=0
        ),
    )(query, near, attn, probs, *rest)


def swap(value, axis):
    return lax.ppermute(value, axis, [(0, 1), (1, 0)])


def up_plane(value):
    return lax.ppermute(value, "z", [(i, (i + 1) % PLANES) for i in range(PLANES)])


def down_plane(value):
    return lax.ppermute(value, "z", [(i, (i - 1) % PLANES) for i in range(PLANES)])


def shifted(value, planes, xl):
    pairs = [
        (2 * i + j, 2 * ((i + planes) % PLANES) + (j + xl) % 2) for i in range(PLANES) for j in range(2)
    ]
    return lax.ppermute(value, ("z", "xl"), pairs)


def body(query, key, value, tile_mask, weight, cot):
    rows, width = query.shape
    f32, bf16 = jnp.float32, jnp.bfloat16
    place = jnp.stack([lax.axis_index("z"), lax.axis_index("xl"), lax.axis_index("core")]).astype(jnp.int32)
    half_weight = lax.all_gather(weight, ("z", "core"), axis=0, tiled=True)
    own = lax.pad(key, jnp.zeros((), bf16), ((0, 0, 0), (0, width, 0)))
    own = own + lax.pad(value, jnp.zeros((), bf16), ((0, 0, 0), (width, 0, 0)))
    from_low, from_high = up_plane(own), down_plane(own)
    own_x = swap(own, "xl")
    far_x = swap(jnp.concatenate([from_low, from_high], axis=0), "xl")
    near_a = jnp.concatenate([own, own_x, from_low, far_x[:rows], from_high, far_x[rows:]], axis=0)
    near_b = swap(near_a, "core")
    attn_out, attn, probs = attend(place, tile_mask, query, near_a, near_b, lax.axis_size(FSDP))
    sides, copies, depth, _ = attn_out.shape
    rows_in = lax.all_to_all(attn_out.reshape(sides * copies, depth, rows), WIDE, 0, 0)
    theirs, held = up_far(place, rows_in, half_weight)
    got = swap(theirs, "xl")
    mine = up_near(place, rows_in, held)
    act, pull, push, pair, sums = middle(mine, got, cot, lax.axis_size(SEQ))
    pair = swap(pair, "xl")
    sums = lax.all_to_all(sums, SEQ, 0, 0)
    back, scales = down(place, pull, push, pair, sums, held)
    scaled = scale(act, scales)
    partial = lax.all_to_all(back, WIDE, 0, 0)
    grad_query, grad_b, grad = backward(1, query, near_b, attn, probs, partial)
    grad_b = swap(grad_b, "core")
    grad_query, grad_a = backward(0, query, near_a, attn, probs, grad, grad_query)
    blocks = [
        grad_a[i * rows : (i + 1) * rows].astype(f32) + grad_b[i * rows : (i + 1) * rows].astype(f32) for i in range(6)
    ]
    moves = ((3, -1, 1), (5, 1, 1), (2, -1, 0), (4, 1, 0), (1, 0, 1))
    arrived = [shifted(blocks[i].astype(bf16), planes, xl) for i, planes, xl in moves]
    terms = [blocks[0]] + [block.astype(f32) for block in arrived]
    grad_key = functools.reduce(jnp.add, [term[:, :width] for term in terms])
    grad_value = functools.reduce(jnp.add, [term[:, width:] for term in terms])
    return scaled, grad_query, grad_key, grad_value


def solution(mesh):
    fine = Mesh(mesh.devices.reshape(PLANES, 2, 2, 4, 2), SEQ + FSDP)
    both = P(SEQ, FSDP)
    return jax.shard_map(
        body,
        mesh=fine,
        in_specs=(both, both, both, P(), both, both),
        out_specs=(both,) * 4,
        check_vma=False,
    )
```

```python
import functools

import jax
import jax.numpy as jnp
from jax import lax
from jax.experimental import pallas as pl
from jax.experimental.pallas import tpu as pltpu
from jax.sharding import Mesh, PartitionSpec as P

HD = 128
TILE = 128
TOKENS = 4096
EPSILON = 1e-05
MASKED = -1e30
ROOT = 0.7978845608028654
CUBIC = 0.044715
PLANES = 8
GROUP = 2
NEAR = ((0, 0), (1, 0), (0, -1), (1, -1), (0, 1), (1, 1))
SEQ = ("z", "xl", "core")
FSDP = ("y", "xh")
WIDE = ("xl", "y", "xh")
NT = (((1,), (1,)), ((), ()))
TN = (((0,), (0,)), ((), ()))
VMEM = pltpu.VMEM
SMEM = pltpu.SMEM


def dot(a, b, dims=(((1,), (0,)), ((), ()))):
    return lax.dot_general(a, b, dims, preferred_element_type=jnp.float32)


def attend_kernel(place, mask, query, near_a, near_b, out, plain, probs, kept, sent):
    z, xl, core = place[0], place[1], place[2]
    me = 4 * z + 2 * xl + core

    def bias_row(other_core):
        parts = []
        for dx, dz in NEAR:
            plane = z + dz
            inside = (plane >= 0) & (plane < PLANES)
            tile = 4 * jnp.clip(plane, 0, PLANES - 1) + 2 * (xl if dx == 0 else 1 - xl) + (1 - core if other_core else core)
            value = jnp.where(inside & (mask[me, tile] > 0), 0.0, MASKED).astype(jnp.float32)
            parts.append(jnp.full((1, TILE), value, jnp.float32))
        return jnp.concatenate(parts, axis=1)

    bias_a, bias_b = bias_row(False), bias_row(True)
    width = near_a.shape[1] // 2
    half = near_a.shape[0]
    scale = HD ** (-0.5)
    for head in range(width // HD):
        cols = slice(head * HD, (head + 1) * HD)
        vcols = slice(width + head * HD, width + (head + 1) * HD)
        q = query[:, cols]
        s_a = dot(q, near_a[:, cols], NT) * scale + bias_a
        s_b = dot(q, near_b[:, cols], NT) * scale + bias_b
        top = jnp.maximum(jnp.max(s_a, axis=1, keepdims=True), jnp.max(s_b, axis=1, keepdims=True))
        e_a = jnp.exp(s_a - top)
        e_b = jnp.exp(s_b - top)
        inv = 1.0 / (jnp.sum(e_a, axis=1, keepdims=True) + jnp.sum(e_b, axis=1, keepdims=True))
        p_a = (e_a * inv).astype(jnp.bfloat16)
        p_b = (e_b * inv).astype(jnp.bfloat16)
        kept[head, :, :half] = p_a
        kept[head, :, half:] = p_b
        pltpu.make_async_copy(kept.at[head], probs.at[head], sent.at[head]).start()
        mixed = dot(p_a, near_a[:, vcols]) + dot(p_b, near_b[:, vcols])
        mixed = mixed.astype(jnp.bfloat16)
        plain[:, cols] = mixed
        turned = mixed.astype(jnp.float32).T.astype(jnp.bfloat16)
        _, copies, lines, tokens = out.shape
        start = head * HD
        while start < (head + 1) * HD:
            side, low = divmod(start, lines)
            stop = min((head + 1) * HD, (side + 1) * lines)
            piece = turned[start - head * HD : stop - head * HD]
            out[side, :, low : low + stop - start, :] = jnp.broadcast_to(piece[None], (copies,) + piece.shape)
            start = stop
    for head in range(width // HD):
        pltpu.make_async_copy(kept.at[head], probs.at[head], sent.at[head]).wait()


def attend(place, mask, query, near_a, near_b, copies):
    rows, width = query.shape
    heads = width // HD
    keys = 2 * near_a.shape[0]
    in_vmem = pl.BlockSpec(memory_space=VMEM)
    return pl.pallas_call(
        attend_kernel,
        out_shape=(
            jax.ShapeDtypeStruct((2, copies, width // 2, rows), jnp.bfloat16),
            jax.ShapeDtypeStruct((rows, width), jnp.bfloat16),
            pltpu.HBM((heads, rows, keys), jnp.bfloat16),
        ),
        in_specs=[pl.BlockSpec(memory_space=SMEM)] * 2 + [in_vmem] * 3,
        out_specs=(in_vmem, in_vmem, pl.BlockSpec(memory_space=pltpu.HBM)),
        scratch_shapes=[pltpu.VMEM((heads, rows, keys), jnp.bfloat16), pltpu.SemaphoreType.DMA((heads,))],
        compiler_params=pltpu.CompilerParams(vmem_limit_bytes=16 << 20),
        cost_estimate=pl.CostEstimate(flops=4 * rows * keys * width, bytes_accessed=8 << 20, transcendentals=heads * rows * keys),
    )(place, mask, query, near_a, near_b)


def turn_kernel(place, rows_in, lhs):
    sides, depth, rows = rows_in.shape
    parts = sides // 2
    for far in range(2):
        side = (1 - place[1]) if far else place[1]
        for first in range(0, parts, GROUP):
            block = rows_in[pl.ds(side * parts + first, GROUP)].reshape(GROUP * depth, rows)
            turned = block.astype(jnp.float32).T.astype(jnp.bfloat16)
            lhs[far, :, first * depth : (first + GROUP) * depth] = turned


def turn(place, rows_in):
    sides, depth, rows = rows_in.shape
    in_vmem = pl.BlockSpec(memory_space=VMEM)
    return pl.pallas_call(
        turn_kernel,
        out_shape=jax.ShapeDtypeStruct((2, rows, sides // 2 * depth), jnp.bfloat16),
        in_specs=[pl.BlockSpec(memory_space=SMEM), in_vmem],
        out_specs=in_vmem,
        compiler_params=pltpu.CompilerParams(vmem_limit_bytes=16 << 20),
        cost_estimate=pl.CostEstimate(flops=0, bytes_accessed=4 * rows_in.size, transcendentals=0),
    )(place, rows_in)


def up_far_kernel(lhs, weight, theirs, held, arrived):
    parts, depth, width = held.shape
    copies = [pltpu.make_async_copy(weight.at[part], held.at[part], arrived.at[part]) for part in range(parts)]
    for copy in copies:
        copy.start()
    total = None
    for first in range(0, parts, GROUP):
        for copy in copies[first : first + GROUP]:
            copy.wait()
        far = lhs[1, :, first * depth : (first + GROUP) * depth]
        term = dot(far, held[first : first + GROUP].reshape(GROUP * depth, width))
        total = term if total is None else total + term
    theirs[...] = total.astype(jnp.bfloat16)


def up_far(lhs, weight):
    _, rows, depth = lhs.shape
    parts = PLANES
    depth = depth // parts
    width = weight.shape[1]
    in_vmem = pl.BlockSpec(memory_space=VMEM)
    in_hbm = pl.BlockSpec(memory_space=pltpu.HBM)
    return pl.pallas_call(
        up_far_kernel,
        out_shape=(
            jax.ShapeDtypeStruct((rows, width), jnp.bfloat16),
            VMEM((parts, depth, width), jnp.bfloat16),
        ),
        in_specs=[in_vmem, in_hbm],
        out_specs=(in_vmem,) * 2,
        scratch_shapes=[pltpu.SemaphoreType.DMA((parts,))],
        compiler_params=pltpu.CompilerParams(vmem_limit_bytes=46 << 20),
        cost_estimate=pl.CostEstimate(
            flops=2 * rows * width * parts * depth, bytes_accessed=weight.size * 2, transcendentals=0
        ),
    )(lhs, weight.reshape(parts, depth, width))


def up_near_kernel(lhs, held, mine):
    parts, depth, width = held.shape
    mine[...] = dot(lhs[0], held[...].reshape(parts * depth, width))


def up_near(lhs, held):
    parts, depth, width = held.shape
    rows = lhs.shape[1]
    in_vmem = pl.BlockSpec(memory_space=VMEM)
    return pl.pallas_call(
        up_near_kernel,
        out_shape=jax.ShapeDtypeStruct((rows, width), jnp.float32),
        in_specs=[in_vmem, in_vmem],
        out_specs=in_vmem,
        compiler_params=pltpu.CompilerParams(vmem_limit_bytes=16 << 20),
        cost_estimate=pl.CostEstimate(
            flops=2 * rows * width * parts * depth, bytes_accessed=held.size * 2, transcendentals=0
        ),
    )(lhs, held)


def middle_kernel(mine, got, cot, act_out, pull_out, push_out, pair, sums):
    chunks = mine.shape[1] // 128
    power, pull = [], []
    for r in range(chunks):
        cols = slice(r * 128, (r + 1) * 128)
        v = mine[:, cols] + got[:, cols].astype(jnp.float32)
        t = jnp.tanh(ROOT * (v + CUBIC * (v * v * v)))
        act = 0.5 * v * (1.0 + t)
        slope = 0.5 * (1.0 + t) + 0.5 * v * (1.0 - t * t) * (ROOT * (1.0 + 3.0 * CUBIC * (v * v)))
        c = cot[:, cols].astype(jnp.float32)
        act_out[:, cols] = act
        pull_out[:, cols] = c * slope
        push_out[:, cols] = act * slope
        pair[0, :, cols] = (c * slope).astype(jnp.bfloat16)
        pair[1, :, cols] = (act * slope).astype(jnp.bfloat16)
        power.append(jnp.sum(act * act, axis=0, keepdims=True))
        pull.append(jnp.sum(act * c, axis=0, keepdims=True))
    lines = power + pull + [jnp.zeros((sums.shape[1] - 2 * chunks, 128), jnp.float32)]
    sums[...] = jnp.broadcast_to(jnp.concatenate(lines, axis=0).astype(jnp.bfloat16)[None], sums.shape)


def middle(mine, got, cot, copies):
    rows, width = mine.shape
    lines = -(-2 * (width // 128) // 8) * 8
    in_vmem = pl.BlockSpec(memory_space=VMEM)
    wide = jax.ShapeDtypeStruct((rows, width), jnp.float32)
    return pl.pallas_call(
        middle_kernel,
        out_shape=(
            wide,
            wide,
            wide,
            jax.ShapeDtypeStruct((2, rows, width), jnp.bfloat16),
            jax.ShapeDtypeStruct((copies, lines, 128), jnp.bfloat16),
        ),
        in_specs=[in_vmem] * 3,
        out_specs=(in_vmem,) * 5,
        compiler_params=pltpu.CompilerParams(vmem_limit_bytes=16 << 20),
        cost_estimate=pl.CostEstimate(flops=40 * rows * width, bytes_accessed=4 << 20, transcendentals=rows * width),
    )(mine, got, cot)


def down_kernel(place, pull, push, pair, sums, weight, out, scales, grad):
    rows, width = pull.shape
    chunks = width // 128
    own = place[1]
    total = jnp.sum(sums[...].astype(jnp.float32), axis=0)
    for r in range(chunks):
        cols = slice(r * 128, (r + 1) * 128)
        inv = lax.rsqrt(total[r : r + 1, :] * (1.0 / TOKENS) + EPSILON)
        back = total[chunks + r : chunks + r + 1, :] * -0.5 * inv * inv * inv * (2.0 / TOKENS)
        scales[r : r + 1, :] = inv
        grad[:rows, cols] = (pull[:, cols] * inv + back * push[:, cols]).astype(jnp.bfloat16)
        far = pair[0, :, cols].astype(jnp.float32) * inv + back * pair[1, :, cols].astype(jnp.float32)
        grad[rows:, cols] = far.astype(jnp.bfloat16)
    parts, depth, _ = weight.shape
    group = 4
    for first in range(0, parts, group):
        term = dot(weight[first : first + group].reshape(group * depth, width), grad[...], NT).astype(jnp.bfloat16)
        out[pl.ds(own * parts + first, group)] = term[:, :rows].reshape(group, depth, rows)
        out[pl.ds((1 - own) * parts + first, group)] = term[:, rows:].reshape(group, depth, rows)


def down(place, pull, push, pair, sums, weight):
    rows, width = pull.shape
    parts, depth, _ = weight.shape
    in_vmem = pl.BlockSpec(memory_space=VMEM)
    return pl.pallas_call(
        down_kernel,
        out_shape=(
            jax.ShapeDtypeStruct((2 * parts, depth, rows), jnp.bfloat16),
            jax.ShapeDtypeStruct((-(-(width // 128) // 8) * 8, 128), jnp.float32),
        ),
        in_specs=[pl.BlockSpec(memory_space=SMEM)] + [in_vmem] * 5,
        out_specs=(in_vmem,) * 2,
        scratch_shapes=[pltpu.VMEM((2 * rows, width), jnp.bfloat16)],
        compiler_params=pltpu.CompilerParams(vmem_limit_bytes=16 << 20),
        cost_estimate=pl.CostEstimate(
            flops=4 * rows * width * parts * depth, bytes_accessed=weight.size * 2, transcendentals=0
        ),
    )(place, pull, push, pair, sums, weight)


def scale_kernel(act, scales, scaled):
    for r in range(act.shape[1] // 128):
        cols = slice(r * 128, (r + 1) * 128)
        scaled[:, cols] = (act[:, cols] * scales[r : r + 1, :]).astype(jnp.bfloat16)


def scale(act, scales):
    in_vmem = pl.BlockSpec(memory_space=VMEM)
    return pl.pallas_call(
        scale_kernel,
        out_shape=jax.ShapeDtypeStruct(act.shape, jnp.bfloat16),
        in_specs=[in_vmem] * 2,
        out_specs=in_vmem,
        compiler_params=pltpu.CompilerParams(vmem_limit_bytes=16 << 20),
        cost_estimate=pl.CostEstimate(flops=act.size, bytes_accessed=6 * act.size, transcendentals=0),
    )(act, scales)


def backward_kernel(side, query, near, attn, probs, *refs):
    if side == 1:
        partial, grad_query, result, kept = refs
        parts = partial.shape[0] // 2
        halves = []
        for x in range(2):
            total = partial[x * parts].astype(jnp.float32)
            for i in range(1, parts):
                total = total + partial[x * parts + i].astype(jnp.float32)
            halves.append(total)
        turned = jnp.concatenate(halves, axis=0)
    else:
        kept, before, grad_query, result = refs
    width = query.shape[1]
    half = near.shape[0]
    scale = HD ** (-0.5)
    for head in range(width // HD):
        cols = slice(head * HD, (head + 1) * HD)
        vcols = slice(width + head * HD, width + (head + 1) * HD)
        if side == 1:
            g = turned[cols].T.astype(jnp.bfloat16)
            kept[:, cols] = g
        else:
            g = kept[:, cols]
        delta = jnp.sum(g.astype(jnp.float32) * attn[:, cols].astype(jnp.float32), axis=1, keepdims=True)
        p = probs[head, :, side * half : (side + 1) * half]
        d = (p.astype(jnp.float32) * (dot(g, near[:, vcols], NT) - delta)).astype(jnp.bfloat16)
        result[:, cols] = (dot(d, query[:, cols], TN) * scale).astype(jnp.bfloat16)
        result[:, vcols] = dot(p, g, TN).astype(jnp.bfloat16)
        term = dot(d, near[:, cols]) * scale
        grad_query[:, cols] = term if side == 1 else before[:, cols] + term


def backward(side, query, near, attn, probs, *rest):
    rows, width = query.shape
    in_vmem = pl.BlockSpec(memory_space=VMEM)
    shapes = [
        jax.ShapeDtypeStruct((rows, width), jnp.float32),
        jax.ShapeDtypeStruct(near.shape, jnp.bfloat16),
    ]
    if side == 1:
        shapes.append(jax.ShapeDtypeStruct((rows, width), jnp.bfloat16))
    return pl.pallas_call(
        functools.partial(backward_kernel, side),
        out_shape=tuple(shapes),
        in_specs=[in_vmem] * (4 + len(rest)),
        out_specs=(in_vmem,) * len(shapes),
        compiler_params=pltpu.CompilerParams(vmem_limit_bytes=16 << 20),
        cost_estimate=pl.CostEstimate(
            flops=8 * rows * near.shape[0] * width, bytes_accessed=4 << 20, transcendentals=0
        ),
    )(query, near, attn, probs, *rest)


def swap(value, axis):
    return lax.ppermute(value, axis, [(0, 1), (1, 0)])


def up_plane(value):
    return lax.ppermute(value, "z", [(i, (i + 1) % PLANES) for i in range(PLANES)])


def down_plane(value):
    return lax.ppermute(value, "z", [(i, (i - 1) % PLANES) for i in range(PLANES)])


def shifted(value, planes, xl):
    pairs = [
        (2 * i + j, 2 * ((i + planes) % PLANES) + (j + xl) % 2) for i in range(PLANES) for j in range(2)
    ]
    return lax.ppermute(value, ("z", "xl"), pairs)


def body(query, key, value, tile_mask, weight, cot):
    rows, width = query.shape
    f32, bf16 = jnp.float32, jnp.bfloat16
    place = jnp.stack([lax.axis_index("z"), lax.axis_index("xl"), lax.axis_index("core")]).astype(jnp.int32)
    half_weight = lax.all_gather(weight, ("z", "core"), axis=0, tiled=True)
    own = lax.pad(key, jnp.zeros((), bf16), ((0, 0, 0), (0, width, 0)))
    own = own + lax.pad(value, jnp.zeros((), bf16), ((0, 0, 0), (width, 0, 0)))
    from_low, from_high = up_plane(own), down_plane(own)
    own_x = swap(own, "xl")
    far_x = swap(jnp.concatenate([from_low, from_high], axis=0), "xl")
    near_a = jnp.concatenate([own, own_x, from_low, far_x[:rows], from_high, far_x[rows:]], axis=0)
    near_b = swap(near_a, "core")
    attn_out, attn, probs = attend(place, tile_mask, query, near_a, near_b, lax.axis_size(FSDP))
    sides, copies, depth, _ = attn_out.shape
    rows_in = lax.all_to_all(attn_out.reshape(sides * copies, depth, rows), WIDE, 0, 0)
    lhs = turn(place, rows_in)
    theirs, held = up_far(lhs, half_weight)
    got = swap(theirs, "xl")
    mine = up_near(lhs, held)
    act, pull, push, pair, sums = middle(mine, got, cot, lax.axis_size(SEQ))
    pair = swap(pair, "xl")
    sums = lax.all_to_all(sums, SEQ, 0, 0)
    back, scales = down(place, pull, push, pair, sums, held)
    scaled = scale(act, scales)
    partial = lax.all_to_all(back, WIDE, 0, 0)
    grad_query, grad_b, grad = backward(1, query, near_b, attn, probs, partial)
    grad_b = swap(grad_b, "core")
    grad_query, grad_a = backward(0, query, near_a, attn, probs, grad, grad_query)
    blocks = [
        grad_a[i * rows : (i + 1) * rows].astype(f32) + grad_b[i * rows : (i + 1) * rows].astype(f32) for i in range(6)
    ]
    moves = ((3, -1, 1), (5, 1, 1), (2, -1, 0), (4, 1, 0), (1, 0, 1))
    arrived = [shifted(blocks[i].astype(bf16), planes, xl) for i, planes, xl in moves]
    terms = [blocks[0]] + [block.astype(f32) for block in arrived]
    grad_key = functools.reduce(jnp.add, [term[:, :width] for term in terms])
    grad_value = functools.reduce(jnp.add, [term[:, width:] for term in terms])
    return scaled, grad_query, grad_key, grad_value


def solution(mesh):
    fine = Mesh(mesh.devices.reshape(PLANES, 2, 2, 4, 2), SEQ + FSDP)
    both = P(SEQ, FSDP)
    return jax.shard_map(
        body,
        mesh=fine,
        in_specs=(both, both, both, P(), both, both),
        out_specs=(both,) * 4,
        check_vma=False,
    )
```

```python
import functools

import jax
import jax.numpy as jnp
from jax import lax
from jax.experimental import pallas as pl
from jax.experimental.pallas import tpu as pltpu
from jax.sharding import Mesh, PartitionSpec as P

HD = 128
TILE = 128
TOKENS = 4096
EPSILON = 1e-05
MASKED = -1e30
ROOT = 0.7978845608028654
CUBIC = 0.044715
PLANES = 8
GROUP = 2
NEAR = ((0, 0), (1, 0), (0, -1), (1, -1), (0, 1), (1, 1))
SEQ = ("z", "xl", "core")
FSDP = ("y", "xh")
WIDE = ("xl", "y", "xh")
NT = (((1,), (1,)), ((), ()))
TN = (((0,), (0,)), ((), ()))
VMEM = pltpu.VMEM
SMEM = pltpu.SMEM


def dot(a, b, dims=(((1,), (0,)), ((), ()))):
    return lax.dot_general(a, b, dims, preferred_element_type=jnp.float32)


def attend_kernel(place, mask, query, near_a, near_b, out, plain, probs, kept, sent):
    z, xl, core = place[0], place[1], place[2]
    me = 4 * z + 2 * xl + core

    def bias_row(other_core):
        parts = []
        for dx, dz in NEAR:
            plane = z + dz
            inside = (plane >= 0) & (plane < PLANES)
            tile = 4 * jnp.clip(plane, 0, PLANES - 1) + 2 * (xl if dx == 0 else 1 - xl) + (1 - core if other_core else core)
            value = jnp.where(inside & (mask[me, tile] > 0), 0.0, MASKED).astype(jnp.float32)
            parts.append(jnp.full((1, TILE), value, jnp.float32))
        return jnp.concatenate(parts, axis=1)

    bias_a, bias_b = bias_row(False), bias_row(True)
    width = near_a.shape[1] // 2
    half = near_a.shape[0]
    scale = HD ** (-0.5)
    for head in range(width // HD):
        cols = slice(head * HD, (head + 1) * HD)
        vcols = slice(width + head * HD, width + (head + 1) * HD)
        q = query[:, cols]
        s_a = dot(q, near_a[:, cols], NT) * scale + bias_a
        s_b = dot(q, near_b[:, cols], NT) * scale + bias_b
        top = jnp.maximum(jnp.max(s_a, axis=1, keepdims=True), jnp.max(s_b, axis=1, keepdims=True))
        e_a = jnp.exp(s_a - top)
        e_b = jnp.exp(s_b - top)
        inv = 1.0 / (jnp.sum(e_a, axis=1, keepdims=True) + jnp.sum(e_b, axis=1, keepdims=True))
        p_a = (e_a * inv).astype(jnp.bfloat16)
        p_b = (e_b * inv).astype(jnp.bfloat16)
        kept[head, :, :half] = p_a
        kept[head, :, half:] = p_b
        pltpu.make_async_copy(kept.at[head], probs.at[head], sent.at[head]).start()
        mixed = dot(p_a, near_a[:, vcols]) + dot(p_b, near_b[:, vcols])
        mixed = mixed.astype(jnp.bfloat16)
        plain[:, cols] = mixed
        turned = mixed.astype(jnp.float32).T.astype(jnp.bfloat16)
        _, copies, lines, tokens = out.shape
        start = head * HD
        while start < (head + 1) * HD:
            side, low = divmod(start, lines)
            stop = min((head + 1) * HD, (side + 1) * lines)
            piece = turned[start - head * HD : stop - head * HD]
            out[side, :, low : low + stop - start, :] = jnp.broadcast_to(piece[None], (copies,) + piece.shape)
            start = stop
    for head in range(width // HD):
        pltpu.make_async_copy(kept.at[head], probs.at[head], sent.at[head]).wait()


def attend(place, mask, query, near_a, near_b, copies):
    rows, width = query.shape
    heads = width // HD
    keys = 2 * near_a.shape[0]
    in_vmem = pl.BlockSpec(memory_space=VMEM)
    return pl.pallas_call(
        attend_kernel,
        out_shape=(
            jax.ShapeDtypeStruct((2, copies, width // 2, rows), jnp.bfloat16),
            jax.ShapeDtypeStruct((rows, width), jnp.bfloat16),
            pltpu.HBM((heads, rows, keys), jnp.bfloat16),
        ),
        in_specs=[pl.BlockSpec(memory_space=SMEM)] * 2 + [in_vmem] * 3,
        out_specs=(in_vmem, in_vmem, pl.BlockSpec(memory_space=pltpu.HBM)),
        scratch_shapes=[pltpu.VMEM((heads, rows, keys), jnp.bfloat16), pltpu.SemaphoreType.DMA((heads,))],
        compiler_params=pltpu.CompilerParams(vmem_limit_bytes=16 << 20),
        cost_estimate=pl.CostEstimate(flops=4 * rows * keys * width, bytes_accessed=8 << 20, transcendentals=heads * rows * keys),
    )(place, mask, query, near_a, near_b)


def turn_kernel(place, rows_in, lhs):
    sides, depth, rows = rows_in.shape
    parts = sides // 2
    for far in range(2):
        side = (1 - place[1]) if far else place[1]
        for first in range(0, parts, GROUP):
            block = rows_in[pl.ds(side * parts + first, GROUP)].reshape(GROUP * depth, rows)
            turned = block.astype(jnp.float32).T.astype(jnp.bfloat16)
            lhs[far, :, first * depth : (first + GROUP) * depth] = turned


def turn(place, rows_in):
    sides, depth, rows = rows_in.shape
    in_vmem = pl.BlockSpec(memory_space=VMEM)
    return pl.pallas_call(
        turn_kernel,
        out_shape=jax.ShapeDtypeStruct((2, rows, sides // 2 * depth), jnp.bfloat16),
        in_specs=[pl.BlockSpec(memory_space=SMEM), in_vmem],
        out_specs=in_vmem,
        compiler_params=pltpu.CompilerParams(vmem_limit_bytes=16 << 20),
        cost_estimate=pl.CostEstimate(flops=0, bytes_accessed=4 * rows_in.size, transcendentals=0),
    )(place, rows_in)


def up_far_kernel(lhs, weight, theirs, held, arrived):
    parts, depth, width = held.shape
    copies = [pltpu.make_async_copy(weight.at[part], held.at[part], arrived.at[part]) for part in range(parts)]
    for copy in copies:
        copy.start()
    total = None
    for first in range(0, parts, GROUP):
        for copy in copies[first : first + GROUP]:
            copy.wait()
        far = lhs[1, :, first * depth : (first + GROUP) * depth]
        term = dot(far, held[first : first + GROUP].reshape(GROUP * depth, width))
        total = term if total is None else total + term
    theirs[...] = total.astype(jnp.bfloat16)


def up_far(lhs, weight):
    _, rows, depth = lhs.shape
    parts = PLANES
    depth = depth // parts
    width = weight.shape[1]
    in_vmem = pl.BlockSpec(memory_space=VMEM)
    in_hbm = pl.BlockSpec(memory_space=pltpu.HBM)
    return pl.pallas_call(
        up_far_kernel,
        out_shape=(
            jax.ShapeDtypeStruct((rows, width), jnp.bfloat16),
            VMEM((parts, depth, width), jnp.bfloat16),
        ),
        in_specs=[in_vmem, in_hbm],
        out_specs=(in_vmem,) * 2,
        scratch_shapes=[pltpu.SemaphoreType.DMA((parts,))],
        compiler_params=pltpu.CompilerParams(vmem_limit_bytes=46 << 20),
        cost_estimate=pl.CostEstimate(
            flops=2 * rows * width * parts * depth, bytes_accessed=weight.size * 2, transcendentals=0
        ),
    )(lhs, weight.reshape(parts, depth, width))


def up_near_kernel(lhs, held, mine):
    parts, depth, width = held.shape
    mine[...] = dot(lhs[0], held[...].reshape(parts * depth, width))


def up_near(lhs, held):
    parts, depth, width = held.shape
    rows = lhs.shape[1]
    in_vmem = pl.BlockSpec(memory_space=VMEM)
    return pl.pallas_call(
        up_near_kernel,
        out_shape=jax.ShapeDtypeStruct((rows, width), jnp.float32),
        in_specs=[in_vmem, in_vmem],
        out_specs=in_vmem,
        compiler_params=pltpu.CompilerParams(vmem_limit_bytes=16 << 20),
        cost_estimate=pl.CostEstimate(
            flops=2 * rows * width * parts * depth, bytes_accessed=held.size * 2, transcendentals=0
        ),
    )(lhs, held)


def middle_kernel(mine, got, cot, act_out, pull_out, push_out, pair, sums):
    chunks = mine.shape[1] // 128
    power, pull = [], []
    for r in range(chunks):
        cols = slice(r * 128, (r + 1) * 128)
        v = mine[:, cols] + got[:, cols].astype(jnp.float32)
        t = jnp.tanh(ROOT * (v + CUBIC * (v * v * v)))
        act = 0.5 * v * (1.0 + t)
        slope = 0.5 * (1.0 + t) + 0.5 * v * (1.0 - t * t) * (ROOT * (1.0 + 3.0 * CUBIC * (v * v)))
        c = cot[:, cols].astype(jnp.float32)
        act_out[:, cols] = act
        pull_out[:, cols] = c * slope
        push_out[:, cols] = act * slope
        pair[0, :, cols] = (c * slope).astype(jnp.bfloat16)
        pair[1, :, cols] = (act * slope).astype(jnp.bfloat16)
        power.append(jnp.sum(act * act, axis=0, keepdims=True))
        pull.append(jnp.sum(act * c, axis=0, keepdims=True))
    lines = power + pull + [jnp.zeros((sums.shape[1] - 2 * chunks, 128), jnp.float32)]
    sums[...] = jnp.broadcast_to(jnp.concatenate(lines, axis=0).astype(jnp.bfloat16)[None], sums.shape)


def middle(mine, got, cot, copies):
    rows, width = mine.shape
    lines = -(-2 * (width // 128) // 8) * 8
    in_vmem = pl.BlockSpec(memory_space=VMEM)
    wide = jax.ShapeDtypeStruct((rows, width), jnp.float32)
    return pl.pallas_call(
        middle_kernel,
        out_shape=(
            wide,
            wide,
            wide,
            jax.ShapeDtypeStruct((2, rows, width), jnp.bfloat16),
            jax.ShapeDtypeStruct((copies, lines, 128), jnp.bfloat16),
        ),
        in_specs=[in_vmem] * 3,
        out_specs=(in_vmem,) * 5,
        compiler_params=pltpu.CompilerParams(vmem_limit_bytes=16 << 20),
        cost_estimate=pl.CostEstimate(flops=40 * rows * width, bytes_accessed=4 << 20, transcendentals=rows * width),
    )(mine, got, cot)


def down_kernel(place, pull, push, pair, sums, weight, out, scales, grad):
    rows, width = pull.shape
    chunks = width // 128
    own = place[1]
    total = jnp.sum(sums[...].astype(jnp.float32), axis=0)
    for r in range(chunks):
        cols = slice(r * 128, (r + 1) * 128)
        inv = lax.rsqrt(total[r : r + 1, :] * (1.0 / TOKENS) + EPSILON)
        back = total[chunks + r : chunks + r + 1, :] * -0.5 * inv * inv * inv * (2.0 / TOKENS)
        scales[r : r + 1, :] = inv
        grad[:rows, cols] = (pull[:, cols] * inv + back * push[:, cols]).astype(jnp.bfloat16)
        far = pair[0, :, cols].astype(jnp.float32) * inv + back * pair[1, :, cols].astype(jnp.float32)
        grad[rows:, cols] = far.astype(jnp.bfloat16)
    parts, depth, _ = weight.shape
    group = 4
    for first in range(0, parts, group):
        term = dot(weight[first : first + group].reshape(group * depth, width), grad[...], NT).astype(jnp.bfloat16)
        out[pl.ds(own * parts + first, group)] = term[:, :rows].reshape(group, depth, rows)
        out[pl.ds((1 - own) * parts + first, group)] = term[:, rows:].reshape(group, depth, rows)


def down(place, pull, push, pair, sums, weight):
    rows, width = pull.shape
    parts, depth, _ = weight.shape
    in_vmem = pl.BlockSpec(memory_space=VMEM)
    return pl.pallas_call(
        down_kernel,
        out_shape=(
            jax.ShapeDtypeStruct((2 * parts, depth, rows), jnp.bfloat16),
            jax.ShapeDtypeStruct((-(-(width // 128) // 8) * 8, 128), jnp.float32),
        ),
        in_specs=[pl.BlockSpec(memory_space=SMEM)] + [in_vmem] * 5,
        out_specs=(in_vmem,) * 2,
        scratch_shapes=[pltpu.VMEM((2 * rows, width), jnp.bfloat16)],
        compiler_params=pltpu.CompilerParams(vmem_limit_bytes=16 << 20),
        cost_estimate=pl.CostEstimate(
            flops=4 * rows * width * parts * depth, bytes_accessed=weight.size * 2, transcendentals=0
        ),
    )(place, pull, push, pair, sums, weight)


def scale_kernel(act, scales, scaled):
    for r in range(act.shape[1] // 128):
        cols = slice(r * 128, (r + 1) * 128)
        scaled[:, cols] = (act[:, cols] * scales[r : r + 1, :]).astype(jnp.bfloat16)


def scale(act, scales):
    in_vmem = pl.BlockSpec(memory_space=VMEM)
    return pl.pallas_call(
        scale_kernel,
        out_shape=jax.ShapeDtypeStruct(act.shape, jnp.bfloat16),
        in_specs=[in_vmem] * 2,
        out_specs=in_vmem,
        compiler_params=pltpu.CompilerParams(vmem_limit_bytes=16 << 20),
        cost_estimate=pl.CostEstimate(flops=act.size, bytes_accessed=6 * act.size, transcendentals=0),
    )(act, scales)


def backward_kernel(side, query, near, attn, probs, *refs):
    if side == 1:
        partial, grad_query, result, kept = refs
        parts = partial.shape[0] // 2
        halves = []
        for x in range(2):
            total = partial[x * parts].astype(jnp.float32)
            for i in range(1, parts):
                total = total + partial[x * parts + i].astype(jnp.float32)
            halves.append(total)
        turned = jnp.concatenate(halves, axis=0)
    else:
        kept, before, grad_query, result = refs
    width = query.shape[1]
    half = near.shape[0]
    scale = HD ** (-0.5)
    for head in range(width // HD):
        cols = slice(head * HD, (head + 1) * HD)
        vcols = slice(width + head * HD, width + (head + 1) * HD)
        if side == 1:
            g = turned[cols].T.astype(jnp.bfloat16)
            kept[:, cols] = g
        else:
            g = kept[:, cols]
        delta = jnp.sum(g.astype(jnp.float32) * attn[:, cols].astype(jnp.float32), axis=1, keepdims=True)
        p = probs[head, :, side * half : (side + 1) * half]
        d = (p.astype(jnp.float32) * (dot(g, near[:, vcols], NT) - delta)).astype(jnp.bfloat16)
        result[:, cols] = (dot(d, query[:, cols], TN) * scale).astype(jnp.bfloat16)
        result[:, vcols] = dot(p, g, TN).astype(jnp.bfloat16)
        term = dot(d, near[:, cols]) * scale
        grad_query[:, cols] = term if side == 1 else before[:, cols] + term


def backward(side, query, near, attn, probs, *rest):
    rows, width = query.shape
    in_vmem = pl.BlockSpec(memory_space=VMEM)
    shapes = [
        jax.ShapeDtypeStruct((rows, width), jnp.float32),
        jax.ShapeDtypeStruct(near.shape, jnp.bfloat16),
    ]
    if side == 1:
        shapes.append(jax.ShapeDtypeStruct((rows, width), jnp.bfloat16))
    return pl.pallas_call(
        functools.partial(backward_kernel, side),
        out_shape=tuple(shapes),
        in_specs=[in_vmem] * (4 + len(rest)),
        out_specs=(in_vmem,) * len(shapes),
        compiler_params=pltpu.CompilerParams(vmem_limit_bytes=16 << 20),
        cost_estimate=pl.CostEstimate(
            flops=8 * rows * near.shape[0] * width, bytes_accessed=4 << 20, transcendentals=0
        ),
    )(query, near, attn, probs, *rest)


def finish_kernel(own, *refs):
    arrived, (grad_key, grad_value) = refs[:-2], refs[-2:]
    width = grad_key.shape[1]
    for out, low in ((grad_key, 0), (grad_value, width)):
        total = own[:, low : low + width]
        for block in arrived:
            total = total + block[:, low : low + width].astype(jnp.float32)
        out[...] = total


def finish(own, *arrived):
    rows, width = own.shape
    in_vmem = pl.BlockSpec(memory_space=VMEM)
    half = jax.ShapeDtypeStruct((rows, width // 2), jnp.float32)
    return pl.pallas_call(
        finish_kernel,
        out_shape=(half, half),
        in_specs=[in_vmem] * (1 + len(arrived)),
        out_specs=(in_vmem,) * 2,
        compiler_params=pltpu.CompilerParams(vmem_limit_bytes=16 << 20),
        cost_estimate=pl.CostEstimate(flops=own.size * len(arrived), bytes_accessed=20 * own.size, transcendentals=0),
    )(own, *arrived)


def swap(value, axis):
    return lax.ppermute(value, axis, [(0, 1), (1, 0)])


def up_plane(value):
    return lax.ppermute(value, "z", [(i, (i + 1) % PLANES) for i in range(PLANES)])


def down_plane(value):
    return lax.ppermute(value, "z", [(i, (i - 1) % PLANES) for i in range(PLANES)])


def shifted(value, planes, xl):
    pairs = [
        (2 * i + j, 2 * ((i + planes) % PLANES) + (j + xl) % 2) for i in range(PLANES) for j in range(2)
    ]
    return lax.ppermute(value, ("z", "xl"), pairs)


def body(query, key, value, tile_mask, weight, cot):
    rows, width = query.shape
    f32, bf16 = jnp.float32, jnp.bfloat16
    place = jnp.stack([lax.axis_index("z"), lax.axis_index("xl"), lax.axis_index("core")]).astype(jnp.int32)
    half_weight = lax.all_gather(weight, ("z", "core"), axis=0, tiled=True)
    own = lax.pad(key, jnp.zeros((), bf16), ((0, 0, 0), (0, width, 0)))
    own = own + lax.pad(value, jnp.zeros((), bf16), ((0, 0, 0), (width, 0, 0)))
    from_low, from_high = up_plane(own), down_plane(own)
    own_x = swap(own, "xl")
    far_x = swap(jnp.concatenate([from_low, from_high], axis=0), "xl")
    near_a = jnp.concatenate([own, own_x, from_low, far_x[:rows], from_high, far_x[rows:]], axis=0)
    near_b = swap(near_a, "core")
    attn_out, attn, probs = attend(place, tile_mask, query, near_a, near_b, lax.axis_size(FSDP))
    sides, copies, depth, _ = attn_out.shape
    rows_in = lax.all_to_all(attn_out.reshape(sides * copies, depth, rows), WIDE, 0, 0)
    lhs = turn(place, rows_in)
    theirs, held = up_far(lhs, half_weight)
    got = swap(theirs, "xl")
    mine = up_near(lhs, held)
    act, pull, push, pair, sums = middle(mine, got, cot, lax.axis_size(SEQ))
    pair = swap(pair, "xl")
    sums = lax.all_to_all(sums, SEQ, 0, 0)
    back, scales = down(place, pull, push, pair, sums, held)
    scaled = scale(act, scales)
    partial = lax.all_to_all(back, WIDE, 0, 0)
    grad_query, grad_b, grad = backward(1, query, near_b, attn, probs, partial)
    grad_b = swap(grad_b, "core")
    grad_query, grad_a = backward(0, query, near_a, attn, probs, grad, grad_query)
    blocks = [
        grad_a[i * rows : (i + 1) * rows].astype(f32) + grad_b[i * rows : (i + 1) * rows].astype(f32) for i in range(6)
    ]
    moves = ((3, -1, 1), (5, 1, 1), (2, -1, 0), (4, 1, 0), (1, 0, 1))
    arrived = [shifted(blocks[i].astype(bf16), planes, xl) for i, planes, xl in moves]
    grad_key, grad_value = finish(blocks[0], *arrived)
    return scaled, grad_query, grad_key, grad_value


def solution(mesh):
    fine = Mesh(mesh.devices.reshape(PLANES, 2, 2, 4, 2), SEQ + FSDP)
    both = P(SEQ, FSDP)
    return jax.shard_map(
        body,
        mesh=fine,
        in_specs=(both, both, both, P(), both, both),
        out_specs=(both,) * 4,
        check_vma=False,
    )
```
